128 devices in a mesh: tok: 8 (over y, z_lo), voc: 16 (over x, z_hi, core).
Axes of the slice: x: 4, y: 4, z: 4 (z_hi: 2, z_lo: 2; z = z_hi * 2 + z_lo), core: 2. Of those that a mesh axis runs over, the one named last changes fastest.
Arguments:
- hidden_states: bfloat16 [1024, 3584], P('tok'), may hold values from -18 to 18
- final_gain: float32 [3584], replicated, may hold values from 0.5 to 1.5
- student_head: bfloat16 [131072, 3584], P(('tok', 'voc')), may hold values from -2 to 2
- teacher_states: bfloat16 [1024, 4608], P('tok'), may hold values from -18 to 18
- teacher_head: bfloat16 [131072, 4608], P(('tok', 'voc')), may hold values from -2 to 2
- token_weight: float32 [1024], replicated, may hold values from 8 to 64
Outputs:
- states_grad: float32 [1024, 3584], P(('tok', 'voc'))
- gain_grad: float32 [3584], replicated
The draws below stay inside these ranges and needn't reach their ends.
All inputs are finite; a program needn't handle non-finite values.
Results may differ from the reference program's by a relative error of at most 0.006.
Values may be sent and summed in bfloat16 or wider, within the bound.
No kernel may reach another device: no remote copies, remote signals or barrier semaphores. Data moves between devices by JAX's collectives and lax.ppermute only.
A program may use at most 128 MiB of HBM per device.

```python
import math
import jax
import jax.numpy as jnp
from jax import lax

DS = 3584
DT = 4608
TOKENS = 1024
VOCAB = 131072


def draw_hidden_states(key, part):
    key = jax.random.fold_in(key, 1)
    key_one = jax.random.fold_in(key, 0)
    values = jnp.clip(jax.random.normal(key_one, (TOKENS, DS), jnp.float32), -4.0, 4.0)
    return values.astype(jnp.bfloat16)


def draw_student_head(key, part):
    key = jax.random.fold_in(key, 2)
    values = jnp.clip(jax.random.normal(key, (VOCAB, DS), jnp.float32), -4.0, 4.0) * (3.0 / math.sqrt(DS))
    return values.astype(jnp.bfloat16)


def draw_teacher_states(key, part):
    key = jax.random.fold_in(key, 3)
    key_one = jax.random.fold_in(key, 0)
    values = jnp.clip(jax.random.normal(key_one, (TOKENS, DT), jnp.float32), -4.0, 4.0)
    return values.astype(jnp.bfloat16)


def draw_teacher_head(key, part):
    key = jax.random.fold_in(key, 4)
    values = jnp.clip(jax.random.normal(key, (VOCAB, DT), jnp.float32), -4.0, 4.0) * (3.0 / math.sqrt(DT))
    return values.astype(jnp.bfloat16)


def setup_inputs(seed: int = 0) -> dict:
    key_of = jax.random.split(jax.random.key(seed), 7)
    hidden_states = draw_hidden_states(jax.random.fold_in(key_of[6], 71), 0)
    final_gain = jnp.clip(1.0 + 0.1 * jax.random.normal(key_of[1], (DS,), jnp.float32), 0.5, 1.5)
    student_head = draw_student_head(jax.random.fold_in(key_of[6], 71), 0)
    teacher_states = draw_teacher_states(jax.random.fold_in(key_of[6], 71), 0)
    teacher_head = draw_teacher_head(jax.random.fold_in(key_of[6], 71), 0)
    token_weight = jnp.clip(jnp.exp(jax.random.uniform(key_of[5], (TOKENS,), jnp.float32, math.log(8.0), math.log(64.0))), 8.0, 64.0)
    return {"hidden_states": hidden_states, "final_gain": final_gain, "student_head": student_head, "teacher_states": teacher_states, "teacher_head": teacher_head, "token_weight": token_weight}


def against(left_side, right_side):
    return lax.dot_general(left_side, right_side, (((1,), (1,)), ((), ())), preferred_element_type=jnp.float32)

def reference(hidden_states, final_gain, student_head, teacher_states, teacher_head, token_weight):
    states_wide = hidden_states.astype(jnp.float32)
    inverse = lax.rsqrt(lax.optimization_barrier(jnp.mean(states_wide * states_wide, axis=1, keepdims=True)) + 1e-06)
    normed = (states_wide * inverse * final_gain).astype(jnp.bfloat16)
    block_rows = math.gcd(TOKENS, 128)
    block_count = TOKENS // block_rows

    def one_block(inputs):
        normed_rows, teacher_rows, weight_rows = inputs
        student_logits = against(normed_rows, student_head)
        teacher_logits = against(teacher_rows, teacher_head)
        student_probs = jax.nn.softmax(student_logits, axis=1)
        teacher_probs = jax.nn.softmax(teacher_logits, axis=1)
        logit_grad = (weight_rows[:, None] * (student_probs - teacher_probs)).astype(jnp.bfloat16)
        return jnp.dot(logit_grad, student_head, preferred_element_type=jnp.float32)
    normed_grad = lax.map(one_block, (normed.reshape(block_count, block_rows, DS), teacher_states.reshape(block_count, block_rows, DT), token_weight.reshape(block_count, block_rows)))
    normed_grad = normed_grad.reshape(TOKENS, DS)
    scaled = normed_grad * final_gain
    states_grad = inverse * scaled - states_wide * inverse ** 3 * lax.optimization_barrier(jnp.mean(states_wide * scaled, axis=1, keepdims=True))
    gain_grad = lax.optimization_barrier(jnp.sum(normed_grad * states_wide * inverse, axis=0))
    return (states_grad, gain_grad)
```

```python
import jax
import jax.numpy as jnp
from jax import lax
from jax.sharding import Mesh, PartitionSpec as P

EPSILON = 1e-06
AXES = ("y", "zl", "x", "zh", "c")
SIZES = (4, 2, 4, 2, 2)
F32 = jnp.float32
BF16 = jnp.bfloat16


def place(y, z, x, c):
    y, z, x, c = y % 4, z % 4, x % 4, c % 2
    return (((y * 2 + z % 2) * 4 + x) * 2 + z // 2) * 2 + c


def permute(array, target):
    pairs = [
        (place(y, z, x, c), place(*target(y, z, x, c)))
        for y in range(4)
        for z in range(4)
        for x in range(4)
        for c in range(2)
    ]
    return lax.ppermute(array, AXES, pairs)


def moved(axis, steps):
    def target(y, z, x, c):
        by = steps if c == 0 else -steps
        name = axis[c]
        return (y + by * (name == "y"), z + by * (name == "z"), x + by * (name == "x"), c)

    return target


def against(left_side, right_side):
    return lax.dot_general(
        left_side, right_side, (((1,), (1,)), ((), ())), preferred_element_type=F32
    )


def pick(rows, columns):
    return rows[:, None] == lax.broadcasted_iota(jnp.int32, (rows.shape[0], columns), 1)


def row_parts(count, *sizes):
    index = lax.iota(jnp.int32, count)
    digits = []
    for size in reversed(sizes):
        digits.append(index % size)
        index = index // size
    return digits[::-1]


def log_sum(parts):
    top = jnp.maximum(jnp.maximum(parts[0], parts[1]), jnp.maximum(parts[2], parts[3]))
    total = sum(jnp.exp(part - top) for part in parts)
    return top + jnp.log(total)


def body(hidden_states, final_gain, student_head, teacher_states, teacher_head, token_weight):
    y, zl, x, zh, c = (lax.axis_index(name) for name in AXES)
    z = zh * 2 + zl
    sign = 1 - 2 * c
    tokens = token_weight.shape[0]
    dt, ds = teacher_states.shape[1], hidden_states.shape[1]
    rows = hidden_states.shape[0] // 2
    unit = rows // 8
    half = tokens // 4

    def swap(array):
        return permute(array, lambda y, z, x, c: (y, z, x, 1 - c))

    kx, kz, i = row_parts(rows, 4, 2, unit)
    source = (((x + sign * kx) % 4 * 2 + (zh ^ kz)) * 2 + c) * unit + i
    select = pick(source, 2 * rows).astype(BF16)
    own = jnp.concatenate(
        [
            jnp.dot(select, states, preferred_element_type=F32).astype(BF16)
            for states in (teacher_states, hidden_states)
        ],
        axis=1,
    )
    teacher_other = swap(teacher_head)
    student_other = swap(student_head)

    from_y = moved(("y", "y"), -1)
    from_z = moved(("z", "z"), -1)
    y1, z0 = permute(own, from_y), permute(own, from_z)
    y2, z1 = permute(y1, from_y), permute(y1, from_z)
    y3, z2 = permute(y2, from_y), permute(y2, from_z)
    cut = (dt + ds) // 2
    z3 = jnp.concatenate(
        [permute(y3[:, :cut], from_z), permute(z2[:, cut:], from_y)], axis=1
    )

    def logits(blocks):
        block = jnp.concatenate(blocks, axis=0)
        teacher, hidden = block[:, :dt], block[:, dt:]
        wide = hidden.astype(F32)
        inverse = lax.rsqrt(jnp.mean(wide * wide, axis=1, keepdims=True) + EPSILON)
        normed = (wide * inverse * final_gain).astype(BF16)
        out = []
        for states, heads in (
            (teacher, (teacher_head, teacher_other)),
            (normed, (student_head, student_other)),
        ):
            pair = [against(states, head) for head in heads]
            top = jnp.maximum(jnp.max(pair[0], axis=1), jnp.max(pair[1], axis=1))
            total = sum(jnp.sum(jnp.exp(part - top[:, None]), axis=1) for part in pair)
            out.append((pair, top + jnp.log(total)))
        return out, hidden, inverse

    halves = [logits([own, z0, y1, z1]), logits([y2, z2, y3, z3])]

    ry, rb, kx, kz, i = row_parts(2 * half, 4, 2, 4, 2, unit)
    rz = kz * 2 + rb
    to_y, to_z, to_x = (y + sign * ry) % 4, (z + sign * rz) % 4, (x + sign * kx) % 4
    absolute = (((to_y * 2 + to_z % 2) * 4 + to_x) * 2 + to_z // 2) * unit + i
    order = pick(absolute, 2 * half).astype(F32)
    token = (absolute // unit * 2 + c) * unit + i
    weight = jnp.sum(jnp.where(pick(token, tokens), token_weight[None, :], 0.0), axis=1)

    local = jnp.stack(
        [jnp.concatenate([part[0][k][1] for part in halves]) for k in range(2)]
    )
    whole = jnp.dot(local, order, precision=lax.Precision.HIGHEST)
    for axis in ("x", "y", "z"):
        whole = log_sum(
            [whole] + [permute(whole, moved((axis, axis), s)) for s in (1, 3, 2)]
        )
    relative = jnp.dot(whole, order.T, precision=lax.Precision.HIGHEST)

    grads = []
    for n, (pairs, _, _) in enumerate(halves):
        span = slice(n * half, (n + 1) * half)
        teacher_lse, student_lse = relative[0, span, None], relative[1, span, None]
        grads.append(
            [
                (
                    weight[span, None]
                    * (jnp.exp(student - student_lse) - jnp.exp(teacher - teacher_lse))
                ).astype(BF16)
                for teacher, student in zip(pairs[0][0], pairs[1][0])
            ]
        )
    grad = jnp.concatenate([jnp.concatenate(pair, axis=1) for pair in grads], axis=0)

    a, b, kz, rb, i = row_parts(2 * half, 4, 4, 2, 2, unit)
    ry, kx = jnp.where(c == 0, b, a), jnp.where(c == 0, a, b)
    send = pick((((ry * 2 + rb) * 4 + kx) * 2 + kz) * unit + i, 2 * half).astype(BF16)
    grad = jnp.dot(send, grad, preferred_element_type=F32).astype(BF16)
    hidden = jnp.concatenate([part[1] for part in halves], axis=0)
    inverse = jnp.concatenate([part[2] for part in halves], axis=0)
    hidden_sent = jnp.dot(send, hidden, preferred_element_type=F32)
    inverse_sent = jnp.dot(send.astype(F32), inverse, precision=lax.Precision.HIGHEST)
    head = jnp.concatenate([student_head, student_other], axis=0)
    partial = jnp.dot(grad, head, preferred_element_type=F32)
    gain = jnp.sum(partial * hidden_sent * inverse_sent, axis=0)

    total = partial
    for axis in (("x", "y"), ("y", "x"), ("z", "z")):
        high = lax.reduce_precision(gain, 8, 7)
        tail = jnp.concatenate(
            [jnp.stack([high, gain - high]).astype(BF16), jnp.zeros((6, ds), BF16)], axis=0
        )
        count = total.shape[0] // 4
        parts = [total[:count]]
        gains = [gain]
        for s in (1, 3, 2):
            piece = jnp.concatenate(
                [total[s * count : (s + 1) * count].astype(BF16), tail], axis=0
            )
            piece = permute(piece, moved(axis, s)).astype(F32)
            parts.append(piece[:count])
            gains.append(piece[count] + piece[count + 1])
        total = (parts[0] + parts[1]) + (parts[2] + parts[3])
        gain = (gains[0] + gains[1]) + (gains[2] + gains[3])
    gain_grad = gain + swap(gain)

    own_states = own[:unit, dt:].astype(F32)
    own_inverse = halves[0][2][:unit]
    scaled = total * final_gain
    states_grad = own_inverse * scaled - own_states * own_inverse**3 * jnp.mean(
        own_states * scaled, axis=1, keepdims=True
    )
    return (states_grad, gain_grad)


def solution(mesh):
    torus = Mesh(mesh.devices.reshape(SIZES), AXES)
    return jax.shard_map(
        body,
        mesh=torus,
        in_specs=(
            P(("y", "zl"), None),
            P(),
            P(AXES, None),
            P(("y", "zl"), None),
            P(AXES, None),
            P(),
        ),
        out_specs=(P(AXES, None), P()),
        check_vma=False,
    )
```

```python
import functools

import jax
import jax.numpy as jnp
from jax import lax
from jax.experimental import pallas as pl
from jax.experimental.pallas import tpu as pltpu
from jax.sharding import Mesh, PartitionSpec as P

EPSILON = 1e-06
AXES = ("y", "zl", "x", "zh", "c")
SIZES = (4, 2, 4, 2, 2)
F32 = jnp.float32
BF16 = jnp.bfloat16


def place(y, z, x, c):
    y, z, x, c = y % 4, z % 4, x % 4, c % 2
    return (((y * 2 + z % 2) * 4 + x) * 2 + z // 2) * 2 + c


def permute(array, target):
    pairs = [
        (place(y, z, x, c), place(*target(y, z, x, c)))
        for y in range(4)
        for z in range(4)
        for x in range(4)
        for c in range(2)
    ]
    return lax.ppermute(array, AXES, pairs)


def moved(axis, steps):
    def target(y, z, x, c):
        by = steps if c == 0 else -steps
        name = axis[c]
        return (y + by * (name == "y"), z + by * (name == "z"), x + by * (name == "x"), c)

    return target


def pick(rows, columns):
    return rows[:, None] == lax.broadcasted_iota(jnp.int32, (rows.shape[0], columns), 1)


def row_parts(count, *sizes):
    index = lax.iota(jnp.int32, count)
    digits = []
    for size in reversed(sizes):
        digits.append(index % size)
        index = index // size
    return digits[::-1]


def log_sum(parts):
    top = jnp.maximum(jnp.maximum(parts[0], parts[1]), jnp.maximum(parts[2], parts[3]))
    total = sum(jnp.exp(part - top) for part in parts)
    return top + jnp.log(total)


def columns_to_rows(columns):
    rows = columns[0].shape[0]
    wide = jnp.concatenate(
        columns + [jnp.zeros((rows, 128 - len(columns)), F32)], axis=1
    )
    return wide.T[:8]


def rows_to_columns(rows):
    count = rows.shape[1]
    return jnp.concatenate([rows, jnp.zeros((120, count), F32)], axis=0).T


def logits_kernel(tile, *refs):
    blocks, (gain, own_t, own_s, other_t, other_s) = refs[:4], refs[4:9]
    out_t, out_s, lse, normed, states_t, wait_t, wait_s, sem = refs[9:]
    rows, dt, vocab = blocks[0].shape[0], states_t.shape[1], own_t.shape[0]
    slots = wait_t.shape[0]
    work = []
    for pair, base in (((own_t, own_s), 0), ((other_t, other_s), vocab)):
        for kind in range(2):
            for first in range(0, vocab, tile):
                work.append((kind, pair[kind], first, base + first))
    copies, slot, used = [], [], [0, 0]
    for kind, head, first, _ in work:
        slot.append(used[kind] % slots)
        used[kind] += 1
        copies.append(
            pltpu.make_async_copy(
                head.at[pl.ds(first, tile)],
                (wait_t, wait_s)[kind].at[slot[-1]],
                sem.at[kind, slot[-1]],
            )
        )
    ahead = slots - 1
    for k in range(ahead):
        copies[k].start()
    for k, block in enumerate(blocks):
        span = pl.ds(k * rows, rows)
        states_t[span, :] = block[:, :dt]
        wide = block[:, dt:].astype(F32)
        inverse = lax.rsqrt(jnp.mean(wide * wide, axis=1, keepdims=True) + EPSILON)
        normed[span, :] = (wide * inverse * gain[...]).astype(BF16)
    count = states_t.shape[0]
    top = [jnp.full((count, 1), -jnp.inf, F32)] * 2
    total = [jnp.zeros((count, 1), F32)] * 2
    outs = (out_t, out_s)

    def statistics(k):
        kind, _, _, base = work[k]
        part = outs[kind][:, pl.ds(base, tile)]
        new = jnp.maximum(top[kind], jnp.max(part, axis=1, keepdims=True))
        total[kind] = total[kind] * jnp.exp(top[kind] - new) + jnp.sum(
            jnp.exp(part - new), axis=1, keepdims=True
        )
        top[kind] = new

    for k, (kind, _, _, base) in enumerate(work):
        copies[k].wait()
        if k + ahead < len(work):
            copies[k + ahead].start()
        outs[kind][:, pl.ds(base, tile)] = lax.dot_general(
            (states_t, normed)[kind][...],
            (wait_t, wait_s)[kind][slot[k]],
            (((1,), (1,)), ((), ())),
            preferred_element_type=F32,
        )
        if k:
            statistics(k - 1)
    statistics(len(work) - 1)
    lse[...] = columns_to_rows([t + jnp.log(z) for t, z in zip(top, total)])


def logits(blocks, gain, own_t, own_s, other_t, other_s):
    count = 4 * blocks[0].shape[0]
    vocab, dt = own_t.shape
    ds = own_s.shape[1]
    tile, slots = 512, 3
    vmem = pl.BlockSpec(memory_space=pltpu.VMEM)
    anywhere = pl.BlockSpec(memory_space=pl.ANY)
    return pl.pallas_call(
        functools.partial(logits_kernel, tile),
        in_specs=[vmem] * 5 + [anywhere] * 4,
        out_specs=[vmem] * 4,
        out_shape=[
            jax.ShapeDtypeStruct((count, 2 * vocab), F32),
            jax.ShapeDtypeStruct((count, 2 * vocab), F32),
            jax.ShapeDtypeStruct((8, count), F32),
            jax.ShapeDtypeStruct((count, ds), BF16),
        ],
        scratch_shapes=[
            pltpu.VMEM((count, dt), BF16),
            pltpu.VMEM((slots, tile, dt), BF16),
            pltpu.VMEM((slots, tile, ds), BF16),
            pltpu.SemaphoreType.DMA((2, slots)),
        ],
        compiler_params=pltpu.CompilerParams(vmem_limit_bytes=58 * 2**20),
        cost_estimate=pl.CostEstimate(
            flops=4 * count * vocab * (dt + ds),
            bytes_accessed=4 * vocab * (dt + ds),
            transcendentals=4 * vocab * count,
        ),
    )(*blocks, gain, own_t, own_s, other_t, other_s)


def backward_kernel(tile, *refs):
    t0, s0, t1, s1, n0, n1, rows, gain, own, other = refs[:10]
    sends, (kept_a, kept_b, gain_out), (grad, head, sem) = refs[10:16], refs[16:19], refs[19:]
    half, vocab = t0.shape
    part, ds = own.shape
    steps = ds // tile
    copies = [
        [
            pltpu.make_async_copy(
                source.at[:, pl.ds(k * tile, tile)],
                head.at[k % 2, pl.ds(n * part, part)],
                sem.at[k % 2, n],
            )
            for n, source in enumerate((own, other))
        ]
        for k in range(steps)
    ]
    for k in range(2):
        for copy in copies[k]:
            copy.start()
    columns = rows_to_columns(rows[...])
    for n, (teacher, student) in enumerate(((t0, s0), (t1, s1))):
        span = slice(n * half, (n + 1) * half)
        lse_t, lse_s, weight = (columns[span, k : k + 1] for k in range(3))
        for first in range(0, vocab, 512):
            at = pl.ds(first, 512)
            gap = jnp.exp(student[:, at] - lse_s) - jnp.exp(teacher[:, at] - lse_t)
            grad[pl.ds(n * half, half), at] = (weight * gap).astype(BF16)
    for k in range(steps):
        for copy in copies[k]:
            copy.wait()
        out = jnp.dot(grad[...], head[k % 2], preferred_element_type=F32)
        if k + 2 < steps:
            for copy in copies[k + 2]:
                copy.start()
        at = pl.ds(k * tile, tile)
        share = jnp.sum(out[:half] * n0[:, at].astype(F32), axis=0, keepdims=True)
        share += jnp.sum(out[half:] * n1[:, at].astype(F32), axis=0, keepdims=True)
        share /= gain[:, at]
        gain_out[:, at] = share
        high = share.astype(BF16).astype(F32)
        tail = jnp.concatenate([high, share - high, jnp.zeros((6, tile), F32)], axis=0)
        second = k >= steps // 2
        at = pl.ds((k - second * (steps // 2)) * tile, tile)
        pieces = []
        for s in range(4):
            if second:
                pieces.append(out[s * 128 : (s + 1) * 128])
            else:
                groups = [out[64 * j + 16 * s : 64 * j + 16 * s + 16] for j in range(8)]
                pieces.append(jnp.concatenate(groups, axis=0))
        (kept_a, kept_b)[second][:, at] = pieces[0]
        for s in range(1, 4):
            sends[3 * second + s - 1][:, at] = jnp.concatenate(
                [pieces[s], tail], axis=0
            ).astype(BF16)


def backward(halves, rows, gain, own, other):
    (t0, s0, _, n0), (t1, s1, _, n1) = halves
    half, vocab = t0.shape
    part, ds = own.shape
    tile = ds // 4
    count = half // 2
    vmem = pl.BlockSpec(memory_space=pltpu.VMEM)
    anywhere = pl.BlockSpec(memory_space=pl.ANY)
    out = pl.pallas_call(
        functools.partial(backward_kernel, tile),
        in_specs=[vmem] * 8 + [anywhere] * 2,
        out_specs=[vmem] * 9,
        out_shape=[jax.ShapeDtypeStruct((count + 8, ds // 2), BF16)] * 6
        + [jax.ShapeDtypeStruct((count, ds // 2), F32)] * 2
        + [jax.ShapeDtypeStruct((1, ds), F32)],
        scratch_shapes=[
            pltpu.VMEM((2 * half, vocab), BF16),
            pltpu.VMEM((2, vocab, tile), BF16),
            pltpu.SemaphoreType.DMA((2, 2)),
        ],
        compiler_params=pltpu.CompilerParams(vmem_limit_bytes=58 * 2**20),
        cost_estimate=pl.CostEstimate(
            flops=4 * half * vocab * ds,
            bytes_accessed=2 * vocab * ds,
            transcendentals=4 * vocab * half,
        ),
    )(t0, s0, t1, s1, n0, n1, rows, gain, own, other)
    return out[:3], out[3:6], out[6], out[7], out[8][0]


def body(hidden_states, final_gain, student_head, teacher_states, teacher_head, token_weight):
    y, zl, x, zh, c = (lax.axis_index(name) for name in AXES)
    z = zh * 2 + zl
    sign = 1 - 2 * c
    tokens = token_weight.shape[0]
    dt, ds = teacher_states.shape[1], hidden_states.shape[1]
    rows = hidden_states.shape[0] // 2
    unit = rows // 8
    half = tokens // 4

    def swap(array):
        return permute(array, lambda y, z, x, c: (y, z, x, 1 - c))

    kx, kz, i = row_parts(rows, 4, 2, unit)
    source = (((x + sign * kx) % 4 * 2 + (zh ^ kz)) * 2 + c) * unit + i
    select = pick(source, 2 * rows).astype(BF16)
    own = jnp.concatenate(
        [
            jnp.dot(select, states, preferred_element_type=F32).astype(BF16)
            for states in (teacher_states, hidden_states)
        ],
        axis=1,
    )
    teacher_other = swap(teacher_head)
    student_other = swap(student_head)

    from_y = moved(("y", "y"), -1)
    from_z = moved(("z", "z"), -1)
    y1, z0 = lax.optimization_barrier((permute(own, from_y), permute(own, from_z)))
    y2, z1 = lax.optimization_barrier((permute(y1, from_y), permute(y1, from_z)))
    y3, z2 = lax.optimization_barrier((permute(y2, from_y), permute(y2, from_z)))
    cut = (dt + ds) // 2
    z3 = jnp.concatenate(
        [permute(y3[:, :cut], from_z), permute(z2[:, cut:], from_y)], axis=1
    )
    gain_row = final_gain[None]
    heads = (teacher_head, student_head, teacher_other, student_other)
    halves = [logits(blocks, gain_row, *heads) for blocks in ([own, z0, y1, z1], [y2, z2, y3, z3])]

    ry, rb, kx, kz, i = row_parts(2 * half, 4, 2, 4, 2, unit)
    rz = kz * 2 + rb
    to_y, to_z, to_x = (y + sign * ry) % 4, (z + sign * rz) % 4, (x + sign * kx) % 4
    absolute = (((to_y * 2 + to_z % 2) * 4 + to_x) * 2 + to_z // 2) * unit + i
    order = pick(absolute, 2 * half).astype(F32)
    token = (absolute // unit * 2 + c) * unit + i
    weight = jnp.sum(jnp.where(pick(token, tokens), token_weight[None, :], 0.0), axis=1)

    local = jnp.concatenate([part[2][:2] for part in halves], axis=1)
    whole = jnp.dot(local, order, precision=lax.Precision.HIGHEST)
    for axis in ("x", "y", "z"):
        whole = log_sum(
            [whole] + [permute(whole, moved((axis, axis), s)) for s in (1, 3, 2)]
        )
    relative = jnp.dot(whole, order.T, precision=lax.Precision.HIGHEST)
    rows = jnp.concatenate([relative, weight[None], jnp.zeros((5, 2 * half), F32)], axis=0)
    sends_a, sends_b, kept_a, kept_b, gain = backward(
        halves, rows, gain_row, student_head, student_other
    )

    def gathered(kept, gain, pieces):
        count = kept.shape[0]
        wide = [piece.astype(F32) for piece in pieces]
        first, second, third = (piece[:count] for piece in wide)
        gains = [piece[count] + piece[count + 1] for piece in wide]
        return (kept + first) + (second + third), (gain + gains[0]) + (gains[1] + gains[2])

    def outgoing(total, gain):
        count = total.shape[0] // 4
        high = lax.reduce_precision(gain, 8, 7)
        tail = jnp.concatenate(
            [jnp.stack([high, gain - high]), jnp.zeros((6, gain.shape[0]), F32)], axis=0
        )
        return total[:count], [
            jnp.concatenate([total[s * count : (s + 1) * count], tail], axis=0).astype(BF16)
            for s in (1, 2, 3)
        ]

    def exchange(pieces, axis):
        moves = {s: permute(pieces[s - 1], moved((axis, axis), s)) for s in (1, 3, 2)}
        return [moves[s] for s in (1, 2, 3)]

    got_a, got_b = exchange(sends_a, "x"), exchange(sends_b, "y")
    total_a, gain_a = gathered(kept_a, gain[: ds // 2], got_a)
    total_b, gain_b = gathered(kept_b, gain[ds // 2 :], got_b)
    total_b = total_b.reshape(2, 4, 2 * unit, ds // 2).swapaxes(0, 1).reshape(total_b.shape)
    kept_a, sends_a = outgoing(total_a, gain_a)
    kept_b, sends_b = outgoing(total_b, gain_b)
    got_a, got_b = exchange(sends_a, "y"), exchange(sends_b, "x")
    total_a, gain_a = gathered(kept_a, gain_a, got_a)
    total_b, gain_b = gathered(kept_b, gain_b, got_b)
    total = jnp.concatenate([total_a, total_b], axis=1)
    total = total.reshape(2, 2, unit, ds).swapaxes(0, 1).reshape(total.shape)
    kept, sends = outgoing(total, jnp.concatenate([gain_a, gain_b]))
    total, gain = gathered(kept, jnp.concatenate([gain_a, gain_b]), exchange(sends, "z"))
    gain_grad = gain + swap(gain)

    own_states = own[:unit, dt:].astype(F32)
    own_inverse = lax.rsqrt(jnp.mean(own_states * own_states, axis=1, keepdims=True) + EPSILON)
    scaled = total * final_gain
    states_grad = own_inverse * scaled - own_states * own_inverse**3 * jnp.mean(
        own_states * scaled, axis=1, keepdims=True
    )
    return (states_grad, gain_grad)


def solution(mesh):
    torus = Mesh(mesh.devices.reshape(SIZES), AXES)
    return jax.shard_map(
        body,
        mesh=torus,
        in_specs=(
            P(("y", "zl"), None),
            P(),
            P(AXES, None),
            P(("y", "zl"), None),
            P(AXES, None),
            P(),
        ),
        out_specs=(P(AXES, None), P()),
        check_vma=False,
    )
```

```python
import functools

import jax
import jax.numpy as jnp
from jax import lax
from jax.experimental import pallas as pl
from jax.experimental.pallas import tpu as pltpu
from jax.sharding import Mesh, PartitionSpec as P

EPSILON = 1e-06
AXES = ("y", "zl", "x", "zh", "c")
SIZES = (4, 2, 4, 2, 2)
F32 = jnp.float32
BF16 = jnp.bfloat16
LOGITS_VMEM = 34 * 2**20
BACKWARD_VMEM = 26 * 2**20


def place(y, z, x, c):
    y, z, x, c = y % 4, z % 4, x % 4, c % 2
    return (((y * 2 + z % 2) * 4 + x) * 2 + z // 2) * 2 + c


def permute(array, target):
    pairs = [
        (place(y, z, x, c), place(*target(y, z, x, c)))
        for y in range(4)
        for z in range(4)
        for x in range(4)
        for c in range(2)
    ]
    return lax.ppermute(array, AXES, pairs)


def moved(axis, steps):
    def target(y, z, x, c):
        by = steps if c == 0 else -steps
        name = axis[c]
        return (y + by * (name == "y"), z + by * (name == "z"), x + by * (name == "x"), c)

    return target


def pick(rows, columns):
    return rows[:, None] == lax.broadcasted_iota(jnp.int32, (rows.shape[0], columns), 1)


def row_parts(count, *sizes):
    index = lax.iota(jnp.int32, count)
    digits = []
    for size in reversed(sizes):
        digits.append(index % size)
        index = index // size
    return digits[::-1]


def columns_to_rows(columns):
    rows = columns[0].shape[0]
    wide = jnp.concatenate(
        columns + [jnp.zeros((rows, 128 - len(columns)), F32)], axis=1
    )
    return wide.T[:8]


def rows_to_columns(rows):
    count = rows.shape[1]
    return jnp.concatenate([rows, jnp.zeros((120, count), F32)], axis=0).T


def logits_kernel(tile, *refs):
    blocks, tail = refs[:-13], refs[-13:]
    gain, own_t, own_s, other_t, other_s, out_t, out_s, lse, normed = tail[:9]
    states_t, wait_t, wait_s, sem = tail[9:]
    rows, dt, vocab = blocks[0].shape[0], states_t.shape[1], own_t.shape[0]
    slots = wait_t.shape[0]
    work = []
    for pair, base in (((own_t, own_s), 0), ((other_t, other_s), vocab)):
        for kind in range(2):
            for first in range(0, vocab, tile):
                work.append((kind, pair[kind], first, base + first))
    copies, slot, used = [], [], [0, 0]
    for kind, head, first, _ in work:
        slot.append(used[kind] % slots)
        used[kind] += 1
        copies.append(
            pltpu.make_async_copy(
                head.at[pl.ds(first, tile)],
                (wait_t, wait_s)[kind].at[slot[-1]],
                sem.at[kind, slot[-1]],
            )
        )
    ahead = slots - 1
    for k in range(ahead):
        copies[k].start()
    for k in range(4):
        span = pl.ds(k * rows, rows)
        block = blocks[k]
        states_t[span, :] = block[:, :dt]
        wide = (blocks[4][...] if block.shape[1] == dt else block[:, dt:]).astype(F32)
        inverse = lax.rsqrt(jnp.mean(wide * wide, axis=1, keepdims=True) + EPSILON)
        normed[span, :] = (wide * inverse * gain[...]).astype(BF16)
    count = states_t.shape[0]
    top = [jnp.full((count, 1), -jnp.inf, F32)] * 2
    total = [jnp.zeros((count, 1), F32)] * 2
    outs = (out_t, out_s)

    def statistics(k):
        kind, _, _, base = work[k]
        part = outs[kind][:, pl.ds(base, tile)]
        new = jnp.maximum(top[kind], jnp.max(part, axis=1, keepdims=True))
        total[kind] = total[kind] * jnp.exp(top[kind] - new) + jnp.sum(
            jnp.exp(part - new), axis=1, keepdims=True
        )
        top[kind] = new

    for k, (kind, _, _, base) in enumerate(work):
        copies[k].wait()
        if k + ahead < len(work):
            copies[k + ahead].start()
        outs[kind][:, pl.ds(base, tile)] = lax.dot_general(
            (states_t, normed)[kind][...],
            (wait_t, wait_s)[kind][slot[k]],
            (((1,), (1,)), ((), ())),
            preferred_element_type=F32,
        )
        if k:
            statistics(k - 1)
    statistics(len(work) - 1)
    lse[...] = columns_to_rows([t + jnp.log(z) for t, z in zip(top, total)])


def logits(blocks, gain, own_t, own_s, other_t, other_s):
    count = 4 * blocks[0].shape[0]
    vocab, dt = own_t.shape
    ds = own_s.shape[1]
    tile, slots = 512, 2
    vmem = pl.BlockSpec(memory_space=pltpu.VMEM)
    anywhere = pl.BlockSpec(memory_space=pl.ANY)
    return pl.pallas_call(
        functools.partial(logits_kernel, tile),
        in_specs=[vmem] * (len(blocks) + 1) + [anywhere] * 4,
        out_specs=[vmem] * 4,
        out_shape=[
            jax.ShapeDtypeStruct((count, 2 * vocab), F32),
            jax.ShapeDtypeStruct((count, 2 * vocab), F32),
            jax.ShapeDtypeStruct((8, count), F32),
            jax.ShapeDtypeStruct((count, ds), BF16),
        ],
        scratch_shapes=[
            pltpu.VMEM((count, dt), BF16),
            pltpu.VMEM((slots, tile, dt), BF16),
            pltpu.VMEM((slots, tile, ds), BF16),
            pltpu.SemaphoreType.DMA((2, slots)),
        ],
        compiler_params=pltpu.CompilerParams(vmem_limit_bytes=LOGITS_VMEM),
        cost_estimate=pl.CostEstimate(
            flops=4 * count * vocab * (dt + ds),
            bytes_accessed=4 * vocab * (dt + ds),
            transcendentals=4 * vocab * count,
        ),
    )(*blocks, gain, own_t, own_s, other_t, other_s)


def backward_kernel(tile, later, *refs):
    teacher, student, normed, rows, gain, own, other = refs[:7]
    before = refs[7] if later else None
    refs = refs[7 + later :]
    sends_a, kept_a, refs = refs[:3], refs[3], refs[4:]
    outs_b, (gain_out, grad, head, sem) = refs[:2], refs[2:]
    half, vocab = teacher.shape
    part, ds = own.shape
    steps = ds // tile
    copies = [
        [
            pltpu.make_async_copy(
                source.at[:, pl.ds(k * tile, tile)],
                head.at[k % 2, pl.ds(n * part, part)],
                sem.at[k % 2, n],
            )
            for n, source in enumerate((own, other))
        ]
        for k in range(steps)
    ]
    for k in range(2):
        for copy in copies[k]:
            copy.start()
    columns = rows_to_columns(rows[...])
    lse_t, lse_s, weight = (columns[:, k : k + 1] for k in range(3))
    for first in range(0, vocab, 512):
        at = pl.ds(first, 512)
        gap = jnp.exp(student[:, at] - lse_s) - jnp.exp(teacher[:, at] - lse_t)
        grad[:, at] = (weight * gap).astype(BF16)
    for k in range(steps):
        for copy in copies[k]:
            copy.wait()
        out = jnp.dot(grad[...], head[k % 2], preferred_element_type=F32)
        if k + 2 < steps:
            for copy in copies[k + 2]:
                copy.start()
        at = pl.ds(k * tile, tile)
        share = jnp.sum(out * normed[:, at].astype(F32), axis=0, keepdims=True)
        share /= gain[:, at]
        gain_out[:, at] = share + before[:, at] if later else share
        second = k >= steps // 2
        at = pl.ds((k - second * (steps // 2)) * tile, tile)
        if second:
            for n in range(2):
                outs_b[n][:, at] = out[n * half // 2 : (n + 1) * half // 2].astype(
                    outs_b[n].dtype
                )
        else:
            for s in range(4):
                groups = [
                    out[64 * j + 16 * s : 64 * j + 16 * s + 16] for j in range(half // 64)
                ]
                piece = jnp.concatenate(groups, axis=0)
                if s == 0:
                    kept_a[:, at] = piece
                else:
                    sends_a[s - 1][pl.ds(0, half // 4), at] = piece.astype(BF16)
    if later:
        share = gain_out[...]
        high = share.astype(BF16).astype(F32)
        low = share - high
        tail = [p[:, n * ds // 2 : (n + 1) * ds // 2] for n in range(2) for p in (high, low)]
        tail = jnp.concatenate(tail + [jnp.zeros((12, ds // 2), F32)], axis=0).astype(BF16)
        for send in sends_a:
            send[pl.ds(half // 4, 16), :] = tail


def backward(part_of, rows, gain, own, other, before=None):
    teacher, student, _, normed = part_of
    later = before is not None
    half, vocab = teacher.shape
    part, ds = own.shape
    tile = ds // 4
    count = half // 4
    vmem = pl.BlockSpec(memory_space=pltpu.VMEM)
    anywhere = pl.BlockSpec(memory_space=pl.ANY)
    wide = ds // 2
    out = pl.pallas_call(
        functools.partial(backward_kernel, tile, later),
        in_specs=[vmem] * 5 + [anywhere] * 2 + [vmem] * later,
        out_specs=[vmem] * 7,
        out_shape=[jax.ShapeDtypeStruct((count + 16 * later, wide), BF16)] * 3
        + [jax.ShapeDtypeStruct((count, wide), F32)]
        + [jax.ShapeDtypeStruct((2 * count, wide), BF16 if later else F32)]
        + [jax.ShapeDtypeStruct((2 * count, wide), BF16)]
        + [jax.ShapeDtypeStruct((1, ds), F32)],
        scratch_shapes=[
            pltpu.VMEM((half, vocab), BF16),
            pltpu.VMEM((2, vocab, tile), BF16),
            pltpu.SemaphoreType.DMA((2, 2)),
        ],
        compiler_params=pltpu.CompilerParams(vmem_limit_bytes=BACKWARD_VMEM),
        cost_estimate=pl.CostEstimate(
            flops=2 * half * vocab * ds,
            bytes_accessed=2 * vocab * ds,
            transcendentals=2 * vocab * half,
        ),
    )(teacher, student, normed, rows, gain, own, other, *([before] if later else []))
    return out[:3], out[3], out[4], out[5], out[6]


def body(hidden_states, final_gain, student_head, teacher_states, teacher_head, token_weight):
    y, zl, x, zh, c = (lax.axis_index(name) for name in AXES)
    z = zh * 2 + zl
    sign = 1 - 2 * c
    tokens = token_weight.shape[0]
    dt, ds = teacher_states.shape[1], hidden_states.shape[1]
    rows = hidden_states.shape[0] // 2
    unit = rows // 8
    half = tokens // 4

    def swap(array):
        return permute(array, lambda y, z, x, c: (y, z, x, 1 - c))

    kx, kz, i = row_parts(rows, 4, 2, unit)
    source = (((x + sign * kx) % 4 * 2 + (zh ^ kz)) * 2 + c) * unit + i
    select = pick(source, 2 * rows).astype(BF16)
    own = jnp.concatenate(
        [
            jnp.dot(select, states, preferred_element_type=F32).astype(BF16)
            for states in (teacher_states, hidden_states)
        ],
        axis=1,
    )
    teacher_other = swap(teacher_head)
    student_other = swap(student_head)

    from_y = moved(("y", "y"), -1)
    from_z = moved(("z", "z"), -1)
    y1, z0 = lax.optimization_barrier((permute(own, from_y), permute(own, from_z)))
    y2, z1 = lax.optimization_barrier((permute(y1, from_y), permute(y1, from_z)))
    gain_row = final_gain[None]
    heads = (teacher_head, student_head, teacher_other, student_other)
    y3, z2 = permute(y2, from_y), permute(y2, from_z)
    first_half = logits([own, z0, y1, z1], gain_row, *heads)
    y3, z2, first_half = lax.optimization_barrier((y3, z2, first_half))
    z3_t, z3_h = permute(y3[:, :dt], from_z), permute(z2[:, dt:], from_y)
    halves = [first_half, logits([y2, z2, y3, z3_t, z3_h], gain_row, *heads)]

    ry, rb, kx, kz, i = row_parts(2 * half, 4, 2, 4, 2, unit)
    rz = kz * 2 + rb
    to_y, to_z, to_x = (y + sign * ry) % 4, (z + sign * rz) % 4, (x + sign * kx) % 4
    absolute = (((to_y * 2 + to_z % 2) * 4 + to_x) * 2 + to_z // 2) * unit + i
    order = pick(absolute, 2 * half).astype(F32)
    token = (absolute // unit * 2 + c) * unit + i
    weight = jnp.sum(jnp.where(pick(token, tokens), token_weight[None, :], 0.0), axis=1)

    local = jnp.concatenate([part[2][:2] for part in halves], axis=1)
    whole = jnp.dot(local, order, precision=lax.Precision.HIGHEST)
    spread = jnp.broadcast_to(whole.reshape(1, 8, -1), (64, 8, half // 2))
    every = lax.all_to_all(spread, AXES[:4], 0, 0, tiled=True)
    top = jnp.max(every, axis=0)
    whole = (top + jnp.log(jnp.sum(jnp.exp(every - top), axis=0))).reshape(whole.shape)
    relative = jnp.dot(whole, order.T, precision=lax.Precision.HIGHEST)
    rows = jnp.concatenate([relative, weight[None], jnp.zeros((5, 2 * half), F32)], axis=0)

    def exchange(pieces, axis):
        moves = {s: permute(pieces[s - 1], moved((axis, axis), s)) for s in (1, 3, 2)}
        return [moves[s].astype(F32) for s in (1, 2, 3)]

    def added(kept, pieces):
        return (kept + pieces[0]) + (pieces[1] + pieces[2])

    def split(array):
        high = lax.reduce_precision(array, 8, 7)
        return high, array - high

    head_pair = (student_head, student_other)
    sends_0, kept_0, kept_b, send_b1, gain_0 = backward(
        halves[0], rows[:, :half], gain_row, *head_pair
    )
    got_0 = exchange(sends_0, "x")
    got_b = [permute(send_b1, moved(("y", "y"), 1)).astype(F32)]
    sends_1, kept_1, send_b2, send_b3, gain_1 = backward(
        halves[1], rows[:, half:], gain_row, *head_pair, gain_0
    )
    got_1 = exchange(sends_1, "x")
    got_b += [
        permute(send, moved(("y", "y"), s)).astype(F32)
        for s, send in ((3, send_b3), (2, send_b2))
    ]
    count = half // 4
    total_a = jnp.concatenate(
        [added(kept_0, got_0), added(kept_1, [piece[:count] for piece in got_1])], axis=0
    )
    total_b = added(kept_b, got_b)

    def gains(tails):
        return [
            jnp.concatenate([tail[0] + tail[1], tail[2] + tail[3]]) for tail in tails
        ]

    gain = added(gain_1[0], gains([piece[count : count + 4] for piece in got_1]))
    wide = ds // 2
    total_b = total_b.reshape(2, 4, 2 * unit, wide).swapaxes(0, 1).reshape(total_b.shape)
    count = total_a.shape[0] // 4
    tail = [p[n * wide : (n + 1) * wide] for n in range(2) for p in split(gain)]
    tail = jnp.concatenate([jnp.stack(tail), jnp.zeros((4, wide), F32)], axis=0)
    pieces_a, pieces_b = (
        [total[s * count : (s + 1) * count] for s in range(4)] for total in (total_a, total_b)
    )
    got_a = exchange(
        [jnp.concatenate([piece, tail], axis=0).astype(BF16) for piece in pieces_a[1:]], "y"
    )
    got_b = exchange([piece.astype(BF16) for piece in pieces_b[1:]], "x")
    total_a = added(pieces_a[0], [piece[:count] for piece in got_a])
    total_b = added(pieces_b[0], got_b)
    gain = added(gain, gains([piece[count : count + 4] for piece in got_a]))
    total = jnp.concatenate([total_a, total_b], axis=1)
    pieces = [total[n * unit : (n + 1) * unit] for n in (0, 2, 1, 3)]
    tail = jnp.concatenate(split(gain)).reshape(unit, -1)
    got = exchange(
        [jnp.concatenate([piece, tail], axis=1).astype(BF16) for piece in pieces[1:]], "z"
    )
    total = added(pieces[0], [piece[:, :ds] for piece in got])
    tails = [piece[:, ds:].reshape(2, ds) for piece in got]
    gain = added(gain, [tail[0] + tail[1] for tail in tails])
    gain_grad = gain + swap(gain)

    own_states = own[:unit, dt:].astype(F32)
    own_inverse = lax.rsqrt(jnp.mean(own_states * own_states, axis=1, keepdims=True) + EPSILON)
    scaled = total * final_gain
    states_grad = own_inverse * scaled - own_states * own_inverse**3 * jnp.mean(
        own_states * scaled, axis=1, keepdims=True
    )
    return (states_grad, gain_grad)


def solution(mesh):
    torus = Mesh(mesh.devices.reshape(SIZES), AXES)
    return jax.shard_map(
        body,
        mesh=torus,
        in_specs=(
            P(("y", "zl"), None),
            P(),
            P(AXES, None),
            P(("y", "zl"), None),
            P(AXES, None),
            P(),
        ),
        out_specs=(P(AXES, None), P()),
        check_vma=False,
    )
```

```python
import functools

import jax
import jax.numpy as jnp
from jax import lax
from jax.experimental import pallas as pl
from jax.experimental.pallas import tpu as pltpu
from jax.sharding import Mesh, PartitionSpec as P

EPSILON = 1e-06
AXES = ("y", "zl", "x", "zh", "c")
SIZES = (4, 2, 4, 2, 2)
F32 = jnp.float32
BF16 = jnp.bfloat16
LARGE = 58 * 2**20


def place(y, z, x, c):
    y, z, x, c = y % 4, z % 4, x % 4, c % 2
    return (((y * 2 + z % 2) * 4 + x) * 2 + z // 2) * 2 + c


def permute(array, target):
    pairs = [
        (place(y, z, x, c), place(*target(y, z, x, c)))
        for y in range(4)
        for z in range(4)
        for x in range(4)
        for c in range(2)
    ]
    return lax.ppermute(array, AXES, pairs)


def moved(axis, steps):
    def target(y, z, x, c):
        by = steps if c == 0 else -steps
        name = axis[c]
        return (y + by * (name == "y"), z + by * (name == "z"), x + by * (name == "x"), c)

    return target


def pick(rows, columns):
    return rows[:, None] == lax.broadcasted_iota(jnp.int32, (rows.shape[0], columns), 1)


def row_parts(count, *sizes):
    index = lax.iota(jnp.int32, count)
    digits = []
    for size in reversed(sizes):
        digits.append(index % size)
        index = index // size
    return digits[::-1]


def columns_to_rows(columns):
    rows = columns[0].shape[0]
    wide = jnp.concatenate(
        columns + [jnp.zeros((rows, 128 - len(columns)), F32)], axis=1
    )
    return wide.T[:8]


def rows_to_columns(rows):
    count = rows.shape[1]
    return jnp.concatenate([rows, jnp.zeros((120, count), F32)], axis=0).T


def logits_kernel(tile, norm, *refs):
    blocks, gain, own, other, out, lse, states, wait, sem = refs[:4], *refs[4:]
    rows, vocab = blocks[0].shape[0], own.shape[0]
    slots, depth = wait.shape[0], states.shape[1]
    work = [(head, first) for head in (own, other) for first in range(0, vocab, tile)]
    copies = [
        pltpu.make_async_copy(
            head.at[pl.ds(first, tile)], wait.at[k % slots], sem.at[k % slots]
        )
        for k, (head, first) in enumerate(work)
    ]
    ahead = slots - 1
    for k in range(ahead):
        copies[k].start()
    for k, block in enumerate(blocks):
        span = pl.ds(k * rows, rows)
        side = pl.ds(0, depth)
        if block.shape[1] > depth and norm:
            side = pl.ds(block.shape[1] - depth, depth)
        if norm:
            wide = block[:, side].astype(F32)
            inverse = lax.rsqrt(jnp.mean(wide * wide, axis=1, keepdims=True) + EPSILON)
            states[span, :] = (wide * inverse * gain[...]).astype(BF16)
        else:
            states[span, :] = block[:, side]
    count = states.shape[0]
    top = jnp.full((count, 1), -jnp.inf, F32)
    total = jnp.zeros((count, 1), F32)

    def statistics(k, top, total):
        part = out[:, pl.ds(k * tile, tile)]
        new = jnp.maximum(top, jnp.max(part, axis=1, keepdims=True))
        total = total * jnp.exp(top - new) + jnp.sum(
            jnp.exp(part - new), axis=1, keepdims=True
        )
        return new, total

    for k in range(len(work)):
        copies[k].wait()
        if k + ahead < len(work):
            copies[k + ahead].start()
        out[:, pl.ds(k * tile, tile)] = lax.dot_general(
            states[...],
            wait[k % slots],
            (((1,), (1,)), ((), ())),
            preferred_element_type=F32,
        )
        if k:
            top, total = statistics(k - 1, top, total)
    top, total = statistics(len(work) - 1, top, total)
    lse[...] = columns_to_rows([top + jnp.log(total)])


def logits(blocks, gain, own, other, norm):
    count = 4 * blocks[0].shape[0]
    vocab, depth = own.shape
    tile, slots = 512, 3
    vmem = pl.BlockSpec(memory_space=pltpu.VMEM)
    anywhere = pl.BlockSpec(memory_space=pl.ANY)
    states = (count, depth)
    return pl.pallas_call(
        functools.partial(logits_kernel, tile, norm),
        in_specs=[vmem] * 5 + [anywhere] * 2,
        out_specs=[vmem] * (2 + norm),
        out_shape=[
            jax.ShapeDtypeStruct((count, 2 * vocab), F32),
            jax.ShapeDtypeStruct((8, count), F32),
        ]
        + [jax.ShapeDtypeStruct(states, BF16)] * norm,
        scratch_shapes=[pltpu.VMEM(states, BF16)] * (not norm)
        + [
            pltpu.VMEM((slots, tile, depth), BF16),
            pltpu.SemaphoreType.DMA((slots,)),
        ],
        compiler_params=pltpu.CompilerParams(vmem_limit_bytes=LARGE),
        cost_estimate=pl.CostEstimate(
            flops=4 * count * vocab * depth,
            bytes_accessed=4 * vocab * depth,
            transcendentals=2 * vocab * count,
        ),
    )(*blocks, gain, own, other)


def backward_kernel(tile, later, *refs):
    teacher, student, normed, rows, gain, own, other = refs[:7]
    before = refs[7] if later else None
    refs = refs[7 + later :]
    sends_a, kept_a, refs = refs[:3], refs[3], refs[4:]
    outs_b, (gain_out, grad, head, sem) = refs[:2], refs[2:]
    half, vocab = teacher.shape
    part, ds = own.shape
    steps = ds // tile
    copies = [
        [
            pltpu.make_async_copy(
                source.at[:, pl.ds(k * tile, tile)],
                head.at[k % 2, pl.ds(n * part, part)],
                sem.at[k % 2, n],
            )
            for n, source in enumerate((own, other))
        ]
        for k in range(steps)
    ]
    for k in range(2):
        for copy in copies[k]:
            copy.start()
    columns = rows_to_columns(rows[...])
    lse_t, lse_s, weight = (columns[:, k : k + 1] for k in range(3))
    for first in range(0, vocab, 512):
        at = pl.ds(first, 512)
        gap = jnp.exp(student[:, at] - lse_s) - jnp.exp(teacher[:, at] - lse_t)
        grad[:, at] = (weight * gap).astype(BF16)
    for k in range(steps):
        for copy in copies[k]:
            copy.wait()
        out = jnp.dot(grad[...], head[k % 2], preferred_element_type=F32)
        if k + 2 < steps:
            for copy in copies[k + 2]:
                copy.start()
        at = pl.ds(k * tile, tile)
        share = jnp.sum(out * normed[:, at].astype(F32), axis=0, keepdims=True)
        share /= gain[:, at]
        gain_out[:, at] = share + before[:, at] if later else share
        second = k >= steps // 2
        at = pl.ds((k - second * (steps // 2)) * tile, tile)
        if second:
            for n in range(2):
                outs_b[n][:, at] = out[n * half // 2 : (n + 1) * half // 2].astype(
                    outs_b[n].dtype
                )
        else:
            for s in range(4):
                groups = [
                    out[64 * j + 16 * s : 64 * j + 16 * s + 16] for j in range(half // 64)
                ]
                piece = jnp.concatenate(groups, axis=0)
                if s == 0:
                    kept_a[:, at] = piece
                else:
                    sends_a[s - 1][pl.ds(0, half // 4), at] = piece.astype(BF16)
    if later:
        share = gain_out[...]
        high = share.astype(BF16).astype(F32)
        low = share - high
        tail = [p[:, n * ds // 2 : (n + 1) * ds // 2] for n in range(2) for p in (high, low)]
        tail = jnp.concatenate(tail + [jnp.zeros((12, ds // 2), F32)], axis=0).astype(BF16)
        for send in sends_a:
            send[pl.ds(half // 4, 16), :] = tail


def backward(part_of, rows, gain, own, other, before=None):
    teacher, student, normed = part_of
    later = before is not None
    half, vocab = teacher.shape
    part, ds = own.shape
    tile = ds // 4
    count = half // 4
    vmem = pl.BlockSpec(memory_space=pltpu.VMEM)
    anywhere = pl.BlockSpec(memory_space=pl.ANY)
    wide = ds // 2
    out = pl.pallas_call(
        functools.partial(backward_kernel, tile, later),
        in_specs=[vmem] * 5 + [anywhere] * 2 + [vmem] * later,
        out_specs=[vmem] * 7,
        out_shape=[jax.ShapeDtypeStruct((count + 16 * later, wide), BF16)] * 3
        + [jax.ShapeDtypeStruct((count, wide), F32)]
        + [jax.ShapeDtypeStruct((2 * count, wide), BF16 if later else F32)]
        + [jax.ShapeDtypeStruct((2 * count, wide), BF16)]
        + [jax.ShapeDtypeStruct((1, ds), F32)],
        scratch_shapes=[
            pltpu.VMEM((half, vocab), BF16),
            pltpu.VMEM((2, vocab, tile), BF16),
            pltpu.SemaphoreType.DMA((2, 2)),
        ],
        compiler_params=pltpu.CompilerParams(vmem_limit_bytes=LARGE),
        cost_estimate=pl.CostEstimate(
            flops=2 * half * vocab * ds,
            bytes_accessed=2 * vocab * ds,
            transcendentals=2 * vocab * half,
        ),
    )(teacher, student, normed, rows, gain, own, other, *([before] if later else []))
    return out[:3], out[3], out[4], out[5], out[6]


def small(kernel, out_shape, *args):
    vmem = pl.BlockSpec(memory_space=pltpu.VMEM)
    return pl.pallas_call(
        kernel,
        in_specs=[vmem] * len(args),
        out_specs=[vmem] * len(out_shape),
        out_shape=[jax.ShapeDtypeStruct(*shape) for shape in out_shape],
        compiler_params=pltpu.CompilerParams(vmem_limit_bytes=LARGE),
    )(*args)


def added(kept, pieces, rows=slice(None)):
    first, second, third = (piece[rows].astype(F32) for piece in pieces)
    return (kept[...] + first) + (second + third)


def tail_rows(gain, count):
    high = gain.astype(BF16).astype(F32)
    low = gain - high
    wide = gain.shape[1] // 2
    rows = [p[:, n * wide : (n + 1) * wide] for n in range(2) for p in (high, low)]
    return jnp.concatenate(rows + [jnp.zeros((count - 4, wide), F32)], axis=0)


def tail_gain(piece, first):
    tail = piece[first : first + 16].astype(F32)
    return jnp.concatenate([tail[0:1] + tail[1:2], tail[2:3] + tail[3:4]], axis=1)


def between_a(*refs):
    kept_0, got_0, kept_1, got_1, gain = refs[0], refs[1:4], refs[4], refs[5:8], refs[8]
    kept, sends, gain_out = refs[9], refs[10:13], refs[13]
    rows = kept_0.shape[0]
    half = rows // 2
    first = added(kept_0, got_0)
    second = added(kept_1, got_1, slice(0, rows))
    gains = [tail_gain(piece, rows) for piece in got_1]
    total = (gain[...] + gains[0]) + (gains[1] + gains[2])
    gain_out[...] = total
    tail = tail_rows(total, 16)
    kept[...] = first[:half]
    for send, piece in zip(sends, (first[half:], second[:half], second[half:])):
        send[...] = jnp.concatenate([piece, tail], axis=0).astype(BF16)


def between_b(*refs):
    total = added(refs[0], refs[1:4])
    half = total.shape[0] // 2
    for s in range(4):
        piece = jnp.concatenate(
            [total[n * half + 16 * s : n * half + 16 * s + 16] for n in range(2)], axis=0
        )
        refs[4 + s][...] = piece.astype(refs[4 + s].dtype)


def before_z(*refs):
    kept_a, got_a, kept_b, got_b, gain = refs[0], refs[1:4], refs[4], refs[5:8], refs[8]
    kept, sends, gain_out = refs[9], refs[10:13], refs[13]
    rows = kept_a.shape[0]
    unit = rows // 4
    total = jnp.concatenate(
        [added(kept_a, got_a, slice(0, rows)), added(kept_b, got_b)], axis=1
    )
    gains = [tail_gain(piece, rows) for piece in got_a]
    share = (gain[...] + gains[0]) + (gains[1] + gains[2])
    gain_out[...] = share
    high = share.astype(BF16).astype(F32)
    tail = jnp.concatenate(
        [high, share - high, jnp.zeros((14 - unit, share.shape[1]), F32)], axis=0
    )
    kept[...] = total[:unit]
    for send, n in zip(sends, (2, 1, 3)):
        piece = total[n * unit : (n + 1) * unit]
        send[...] = jnp.concatenate([piece, tail], axis=0).astype(BF16)


def last_gain(kept, first, second, third, out):
    unit = first.shape[0] // 2
    tails = [piece[...].astype(F32)[unit:] for piece in (first, second, third)]
    shares = [tail[0:1] + tail[1:2] for tail in tails]
    out[...] = (kept[...] + shares[0]) + (shares[1] + shares[2])


def last_states(kept, first, second, third, states, gain, out):
    unit = kept.shape[0]
    pieces = [piece[...].astype(F32)[:unit] for piece in (first, second, third)]
    total = (kept[...] + pieces[0]) + (pieces[1] + pieces[2])
    own = states[...]
    inverse = lax.rsqrt(jnp.mean(own * own, axis=1, keepdims=True) + EPSILON)
    scaled = total * gain[...]
    out[...] = inverse * scaled - own * (inverse * inverse * inverse) * jnp.mean(
        own * scaled, axis=1, keepdims=True
    )


def body(hidden_states, final_gain, student_head, teacher_states, teacher_head, token_weight):
    y, zl, x, zh, c = (lax.axis_index(name) for name in AXES)
    z = zh * 2 + zl
    sign = 1 - 2 * c
    tokens = token_weight.shape[0]
    dt, ds = teacher_states.shape[1], hidden_states.shape[1]
    rows = hidden_states.shape[0] // 2
    unit = rows // 8
    half = tokens // 4

    def swap(array):
        return permute(array, lambda y, z, x, c: (y, z, x, 1 - c))

    kx, kz, i = row_parts(rows, 4, 2, unit)
    source = (((x + sign * kx) % 4 * 2 + (zh ^ kz)) * 2 + c) * unit + i
    select = pick(source, 2 * rows).astype(BF16)
    own = jnp.concatenate(
        [
            jnp.dot(select, states, preferred_element_type=F32).astype(BF16)
            for states in (teacher_states, hidden_states)
        ],
        axis=1,
    )
    teacher_other = swap(teacher_head)
    student_other = swap(student_head)

    from_y = moved(("y", "y"), -1)
    from_z = moved(("z", "z"), -1)
    y1, z0 = lax.optimization_barrier((permute(own, from_y), permute(own, from_z)))
    y2, z1 = lax.optimization_barrier((permute(y1, from_y), permute(y1, from_z)))
    gain_row = final_gain[None]
    y3, z2 = permute(y2, from_y), permute(y2, from_z)
    near, far = [own, z0, y1, z1], [y2, z2, y3]
    teacher_0, lse_t0 = logits(near, gain_row, teacher_head, teacher_other, False)
    y3, z2, teacher_0, lse_t0 = lax.optimization_barrier((y3, z2, teacher_0, lse_t0))
    far = [y2, z2, y3]
    z3_t, z3_h = permute(y3[:, :dt], from_z), permute(z2[:, dt:], from_y)
    student_0, lse_s0, normed_0 = logits(near, gain_row, student_head, student_other, True)
    z3_t, z3_h, student_0, lse_s0, normed_0 = lax.optimization_barrier(
        (z3_t, z3_h, student_0, lse_s0, normed_0)
    )
    teacher_1, lse_t1 = logits(far + [z3_t], gain_row, teacher_head, teacher_other, False)
    student_1, lse_s1, normed_1 = logits(
        far + [z3_h], gain_row, student_head, student_other, True
    )
    halves = [(teacher_0, student_0, normed_0), (teacher_1, student_1, normed_1)]

    ry, rb, kx, kz, i = row_parts(2 * half, 4, 2, 4, 2, unit)
    rz = kz * 2 + rb
    to_y, to_z, to_x = (y + sign * ry) % 4, (z + sign * rz) % 4, (x + sign * kx) % 4
    absolute = (((to_y * 2 + to_z % 2) * 4 + to_x) * 2 + to_z // 2) * unit + i
    order = pick(absolute, 2 * half).astype(F32)
    token = (absolute // unit * 2 + c) * unit + i
    weight = jnp.sum(jnp.where(pick(token, tokens), token_weight[None, :], 0.0), axis=1)

    local = jnp.stack(
        [jnp.concatenate([lse_t0[0], lse_t1[0]]), jnp.concatenate([lse_s0[0], lse_s1[0]])]
    )
    whole = jnp.dot(local, order, precision=lax.Precision.HIGHEST)
    spread = jnp.broadcast_to(whole.reshape(1, 8, -1), (64, 8, half // 2))
    every = lax.all_to_all(spread, AXES[:4], 0, 0, tiled=True)
    top = jnp.max(every, axis=0)
    whole = (top + jnp.log(jnp.sum(jnp.exp(every - top), axis=0))).reshape(whole.shape)
    relative = jnp.dot(whole, order.T, precision=lax.Precision.HIGHEST)
    rows = jnp.concatenate([relative, weight[None], jnp.zeros((5, 2 * half), F32)], axis=0)

    def exchange(pieces, axis):
        moves = {s: permute(pieces[s - 1], moved((axis, axis), s)) for s in (1, 3, 2)}
        return [moves[s] for s in (1, 2, 3)]

    head_pair = (student_head, student_other)
    sends_0, kept_0, kept_b, send_b1, gain_0 = backward(
        halves[0], rows[:, :half], gain_row, *head_pair
    )
    got_0 = exchange(sends_0, "x")
    got_b1 = permute(send_b1, moved(("y", "y"), 1))
    sends_1, kept_1, send_b2, send_b3, gain = backward(
        halves[1], rows[:, half:], gain_row, *head_pair, gain_0
    )
    got_1 = exchange(sends_1, "x")
    got_b3 = permute(send_b3, moved(("y", "y"), 3))
    got_b2 = permute(send_b2, moved(("y", "y"), 2))
    wide = ds // 2
    count = half // 8
    kept_a, *sends_a, gain = small(
        between_a,
        [((count, wide), F32)] + [((count + 16, wide), BF16)] * 3 + [((1, ds), F32)],
        *(kept_0, *got_0, kept_1, *got_1, gain),
    )
    got_a = exchange(sends_a, "y")
    kept_b, *sends_b = small(
        between_b,
        [((count, wide), F32)] + [((count, wide), BF16)] * 3,
        *(kept_b, got_b1, got_b2, got_b3),
    )
    got_b = exchange(sends_b, "x")
    kept, *sends, gain = small(
        before_z,
        [((unit, ds), F32)] + [((16, ds), BF16)] * 3 + [((1, ds), F32)],
        *(kept_a, *got_a, kept_b, *got_b, gain),
    )
    got = exchange(sends, "z")
    (gain,) = small(last_gain, [((1, ds), F32)], gain, *got)
    gain_grad = (gain + swap(gain))[0]
    (states_grad,) = small(
        last_states, [((unit, ds), F32)], kept, *got, own[:unit, dt:].astype(F32), gain_row
    )
    return (states_grad, gain_grad)


def solution(mesh):
    torus = Mesh(mesh.devices.reshape(SIZES), AXES)
    return jax.shard_map(
        body,
        mesh=torus,
        in_specs=(
            P(("y", "zl"), None),
            P(),
            P(AXES, None),
            P(("y", "zl"), None),
            P(AXES, None),
            P(),
        ),
        out_specs=(P(AXES, None), P()),
        check_vma=False,
    )
```

```python
import functools

import jax
import jax.numpy as jnp
from jax import lax
from jax.experimental import pallas as pl
from jax.experimental.pallas import tpu as pltpu
from jax.sharding import Mesh, PartitionSpec as P

EPSILON = 1e-06
AXES = ("y", "zl", "x", "zh", "c")
SIZES = (4, 2, 4, 2, 2)
F32 = jnp.float32
BF16 = jnp.bfloat16
STREAMED = 58 * 2**20
LARGE = 30 * 2**20
SMALL = 3 * 2**20


def place(y, z, x, c):
    y, z, x, c = y % 4, z % 4, x % 4, c % 2
    return (((y * 2 + z % 2) * 4 + x) * 2 + z // 2) * 2 + c


def permute(array, target):
    pairs = [
        (place(y, z, x, c), place(*target(y, z, x, c)))
        for y in range(4)
        for z in range(4)
        for x in range(4)
        for c in range(2)
    ]
    return lax.ppermute(array, AXES, pairs)


def moved(axis, steps):
    def target(y, z, x, c):
        by = steps if c == 0 else -steps
        name = axis[c]
        return (y + by * (name == "y"), z + by * (name == "z"), x + by * (name == "x"), c)

    return target


def pick(rows, columns):
    return rows[:, None] == lax.broadcasted_iota(jnp.int32, (rows.shape[0], columns), 1)


def row_parts(count, *sizes):
    index = lax.iota(jnp.int32, count)
    digits = []
    for size in reversed(sizes):
        digits.append(index % size)
        index = index // size
    return digits[::-1]


def columns_to_rows(columns):
    rows = columns[0].shape[0]
    wide = jnp.concatenate(
        columns + [jnp.zeros((rows, 128 - len(columns)), F32)], axis=1
    )
    return wide.T[:8]


def rows_to_columns(rows):
    count = rows.shape[1]
    return jnp.concatenate([rows, jnp.zeros((120, count), F32)], axis=0).T


def resident_kernel(*refs):
    count = (len(refs) - 1) // 2
    sem = refs[-1]
    copies = [
        pltpu.make_async_copy(refs[n], refs[count + n], sem.at[n]) for n in range(count)
    ]
    for copy in copies:
        copy.start()
    for copy in copies:
        copy.wait()


def resident(*arrays):
    return pl.pallas_call(
        resident_kernel,
        in_specs=[pl.BlockSpec(memory_space=pl.ANY)] * len(arrays),
        out_specs=[pl.BlockSpec(memory_space=pltpu.VMEM)] * len(arrays),
        out_shape=[pltpu.VMEM(array.shape, array.dtype) for array in arrays],
        scratch_shapes=[pltpu.SemaphoreType.DMA((len(arrays),))],
        compiler_params=pltpu.CompilerParams(vmem_limit_bytes=SMALL),
        cost_estimate=pl.CostEstimate(
            flops=0, bytes_accessed=4 * sum(a.size for a in arrays), transcendentals=0
        ),
    )(*[pltpu.with_memory_space_constraint(array, pltpu.HBM) for array in arrays])


def logits_kernel(tile, *refs):
    blocks, refs = refs[:-12], refs[-12:]
    gain, own_t, own_s, other_t, other_s, out_t, out_s, lse, normed, states_t, wait, sem = refs
    rows, vocab, dt = blocks[0].shape[0], own_t.shape[0], own_t.shape[1]
    slots = wait.shape[0]
    copies = [
        pltpu.make_async_copy(
            head.at[pl.ds(first, tile)], wait.at[n % slots], sem.at[n % slots]
        )
        for n, (head, first) in enumerate(
            (head, first) for head in (own_t, other_t) for first in range(0, vocab, tile)
        )
    ]
    for n in range(slots):
        copies[n].start()
    for k in range(4):
        span = pl.ds(k * rows, rows)
        block = blocks[k]
        states_t[span, :] = block[:, :dt]
        wide = (block[:, dt:] if block.shape[1] > dt else blocks[4][...]).astype(F32)
        inverse = lax.rsqrt(jnp.mean(wide * wide, axis=1, keepdims=True) + EPSILON)
        normed[span, :] = (wide * inverse * gain[...]).astype(BF16)
    count = states_t.shape[0]

    def statistics(out, n, top, total):
        part = out[:, pl.ds(n * tile, tile)]
        new = jnp.maximum(top, jnp.max(part, axis=1, keepdims=True))
        total = total * jnp.exp(top - new) + jnp.sum(
            jnp.exp(part - new), axis=1, keepdims=True
        )
        return new, total

    sums = []
    for states, out in ((normed, out_s), (states_t, out_t)):
        top = jnp.full((count, 1), -jnp.inf, F32)
        total = jnp.zeros((count, 1), F32)
        for n in range(2 * vocab // tile):
            if out is out_s:
                head = (own_s, other_s)[n * tile // vocab]
                head = head[pl.ds(n * tile % vocab, tile), :]
            else:
                copies[n].wait()
                head = wait[n % slots]
            out[:, pl.ds(n * tile, tile)] = lax.dot_general(
                states[...], head, (((1,), (1,)), ((), ())), preferred_element_type=F32
            )
            if out is out_t and n + slots < len(copies):
                copies[n + slots].start()
            if n:
                top, total = statistics(out, n - 1, top, total)
        top, total = statistics(out, 2 * vocab // tile - 1, top, total)
        sums.append(top + jnp.log(total))
    lse[...] = columns_to_rows(sums[::-1])


def streamed_kernel(tile, *refs):
    blocks, (gain, own_t, own_s, other_t, other_s) = refs[:4], refs[4:9]
    out_t, out_s, lse, normed, states_t, wait_t, wait_s, sem = refs[9:]
    rows, dt, vocab = blocks[0].shape[0], states_t.shape[1], own_t.shape[0]
    slots = wait_t.shape[0]
    work = []
    for pair, base in (((own_t, own_s), 0), ((other_t, other_s), vocab)):
        for kind in range(2):
            for first in range(0, vocab, tile):
                work.append((kind, pair[kind], first, base + first))
    copies, slot, used = [], [], [0, 0]
    for kind, head, first, _ in work:
        slot.append(used[kind] % slots)
        used[kind] += 1
        copies.append(
            pltpu.make_async_copy(
                head.at[pl.ds(first, tile)],
                (wait_t, wait_s)[kind].at[slot[-1]],
                sem.at[kind, slot[-1]],
            )
        )
    ahead = slots - 1
    for k in range(ahead):
        copies[k].start()
    for k, block in enumerate(blocks):
        span = pl.ds(k * rows, rows)
        states_t[span, :] = block[:, :dt]
        wide = block[:, dt:].astype(F32)
        inverse = lax.rsqrt(jnp.mean(wide * wide, axis=1, keepdims=True) + EPSILON)
        normed[span, :] = (wide * inverse * gain[...]).astype(BF16)
    count = states_t.shape[0]
    top = [jnp.full((count, 1), -jnp.inf, F32)] * 2
    total = [jnp.zeros((count, 1), F32)] * 2
    outs = (out_t, out_s)

    def statistics(k):
        kind, _, _, base = work[k]
        part = outs[kind][:, pl.ds(base, tile)]
        new = jnp.maximum(top[kind], jnp.max(part, axis=1, keepdims=True))
        total[kind] = total[kind] * jnp.exp(top[kind] - new) + jnp.sum(
            jnp.exp(part - new), axis=1, keepdims=True
        )
        top[kind] = new

    for k, (kind, _, _, base) in enumerate(work):
        copies[k].wait()
        if k + ahead < len(work):
            copies[k + ahead].start()
        outs[kind][:, pl.ds(base, tile)] = lax.dot_general(
            (states_t, normed)[kind][...],
            (wait_t, wait_s)[kind][slot[k]],
            (((1,), (1,)), ((), ())),
            preferred_element_type=F32,
        )
        if k:
            statistics(k - 1)
    statistics(len(work) - 1)
    lse[...] = columns_to_rows([t + jnp.log(z) for t, z in zip(top, total)])


def logits_streamed(blocks, gain, own_t, own_s, other_t, other_s):
    count = 4 * blocks[0].shape[0]
    vocab, dt = own_t.shape
    ds = own_s.shape[1]
    tile, slots = 512, 3
    vmem = pl.BlockSpec(memory_space=pltpu.VMEM)
    anywhere = pl.BlockSpec(memory_space=pl.ANY)
    return pl.pallas_call(
        functools.partial(streamed_kernel, tile),
        in_specs=[vmem] * 5 + [anywhere] * 4,
        out_specs=[vmem] * 4,
        out_shape=[
            jax.ShapeDtypeStruct((count, 2 * vocab), F32),
            jax.ShapeDtypeStruct((count, 2 * vocab), F32),
            jax.ShapeDtypeStruct((8, count), F32),
            jax.ShapeDtypeStruct((count, ds), BF16),
        ],
        scratch_shapes=[
            pltpu.VMEM((count, dt), BF16),
            pltpu.VMEM((slots, tile, dt), BF16),
            pltpu.VMEM((slots, tile, ds), BF16),
            pltpu.SemaphoreType.DMA((2, slots)),
        ],
        compiler_params=pltpu.CompilerParams(vmem_limit_bytes=STREAMED),
        cost_estimate=pl.CostEstimate(
            flops=4 * count * vocab * (dt + ds),
            bytes_accessed=4 * vocab * (dt + ds),
            transcendentals=4 * vocab * count,
        ),
    )(*blocks, gain, own_t, own_s, other_t, other_s)


def held(array):
    return pltpu.with_memory_space_constraint(array, pltpu.VMEM)


def logits(blocks, gain, own_t, own_s, other_t, other_s):
    count = 4 * blocks[0].shape[0]
    vocab, dt = own_t.shape
    ds = own_s.shape[1]
    tile, slots = 512, 2
    vmem = pl.BlockSpec(memory_space=pltpu.VMEM)
    anywhere = pl.BlockSpec(memory_space=pl.ANY)
    return pl.pallas_call(
        functools.partial(logits_kernel, tile),
        in_specs=[vmem] * (len(blocks) + 1) + [anywhere, vmem] * 2,
        out_specs=[vmem] * 4,
        out_shape=[
            jax.ShapeDtypeStruct((count, 2 * vocab), F32),
            jax.ShapeDtypeStruct((count, 2 * vocab), F32),
            jax.ShapeDtypeStruct((8, count), F32),
            jax.ShapeDtypeStruct((count, ds), BF16),
        ],
        scratch_shapes=[
            pltpu.VMEM((count, dt), BF16),
            pltpu.VMEM((slots, tile, dt), BF16),
            pltpu.SemaphoreType.DMA((slots,)),
        ],
        compiler_params=pltpu.CompilerParams(vmem_limit_bytes=LARGE),
        cost_estimate=pl.CostEstimate(
            flops=4 * count * vocab * (dt + ds),
            bytes_accessed=4 * vocab * (dt + ds),
            transcendentals=4 * vocab * count,
        ),
    )(*blocks, gain, own_t, held(own_s), other_t, held(other_s))


def backward_kernel(tile, later, *refs):
    teacher, student, normed, rows, gain, own, other = refs[:7]
    before = refs[7] if later else None
    refs = refs[7 + later :]
    sends_a, kept_a, refs = refs[:3], refs[3], refs[4:]
    outs_b, (gain_out, grad) = refs[:2], refs[2:]
    half, vocab = teacher.shape
    part, ds = own.shape
    steps = ds // tile
    columns = rows_to_columns(rows[...])
    lse_t, lse_s, weight = (columns[:, k : k + 1] for k in range(3))
    for first in range(0, vocab, 512):
        at = pl.ds(first, 512)
        gap = jnp.exp(student[:, at] - lse_s) - jnp.exp(teacher[:, at] - lse_t)
        grad[:, at] = (weight * gap).astype(BF16)
    for k in range(steps):
        at = pl.ds(k * tile, tile)
        out = jnp.dot(grad[:, :part], own[:, at], preferred_element_type=F32)
        out += jnp.dot(grad[:, part:], other[:, at], preferred_element_type=F32)
        share = jnp.sum(out * normed[:, at].astype(F32), axis=0, keepdims=True)
        share /= gain[:, at]
        gain_out[:, at] = share + before[:, at] if later else share
        second = k >= steps // 2
        at = pl.ds((k - second * (steps // 2)) * tile, tile)
        if second:
            for n in range(2):
                outs_b[n][:, at] = out[n * half // 2 : (n + 1) * half // 2].astype(
                    outs_b[n].dtype
                )
        else:
            for s in range(4):
                groups = [
                    out[64 * j + 16 * s : 64 * j + 16 * s + 16] for j in range(half // 64)
                ]
                piece = jnp.concatenate(groups, axis=0)
                if s == 0:
                    kept_a[:, at] = piece
                else:
                    sends_a[s - 1][pl.ds(0, half // 4), at] = piece.astype(BF16)
    if later:
        share = gain_out[...]
        high = share.astype(BF16).astype(F32)
        low = share - high
        tail = [p[:, n * ds // 2 : (n + 1) * ds // 2] for n in range(2) for p in (high, low)]
        tail = jnp.concatenate(tail + [jnp.zeros((12, ds // 2), F32)], axis=0).astype(BF16)
        for send in sends_a:
            send[pl.ds(half // 4, 16), :] = tail


def backward(part_of, rows, gain, own, other, before=None):
    teacher, student, _, normed = part_of
    later = before is not None
    half, vocab = teacher.shape
    part, ds = own.shape
    tile = ds // 4
    count = half // 4
    vmem = pl.BlockSpec(memory_space=pltpu.VMEM)
    wide = ds // 2
    out = pl.pallas_call(
        functools.partial(backward_kernel, tile, later),
        in_specs=[vmem] * (7 + later),
        out_specs=[vmem] * 7,
        out_shape=[jax.ShapeDtypeStruct((count + 16 * later, wide), BF16)] * 3
        + [jax.ShapeDtypeStruct((count, wide), F32)]
        + [jax.ShapeDtypeStruct((2 * count, wide), BF16 if later else F32)]
        + [jax.ShapeDtypeStruct((2 * count, wide), BF16)]
        + [jax.ShapeDtypeStruct((1, ds), F32)],
        scratch_shapes=[pltpu.VMEM((half, vocab), BF16)],
        compiler_params=pltpu.CompilerParams(vmem_limit_bytes=SMALL),
        cost_estimate=pl.CostEstimate(
            flops=2 * half * vocab * ds,
            bytes_accessed=2 * vocab * ds,
            transcendentals=2 * vocab * half,
        ),
    )(teacher, student, normed, rows, gain, held(own), held(other), *([before] if later else []))
    return out[:3], out[3], out[4], out[5], out[6]


def small(kernel, out_shape, *args):
    vmem = pl.BlockSpec(memory_space=pltpu.VMEM)
    return pl.pallas_call(
        kernel,
        in_specs=[vmem] * len(args),
        out_specs=[vmem] * len(out_shape),
        out_shape=[jax.ShapeDtypeStruct(*shape) for shape in out_shape],
        compiler_params=pltpu.CompilerParams(vmem_limit_bytes=SMALL),
    )(*args)


def added(kept, pieces, rows=slice(None)):
    first, second, third = (piece[rows].astype(F32) for piece in pieces)
    return (kept[...] + first) + (second + third)


def tail_rows(gain, count):
    high = gain.astype(BF16).astype(F32)
    low = gain - high
    wide = gain.shape[1] // 2
    rows = [p[:, n * wide : (n + 1) * wide] for n in range(2) for p in (high, low)]
    return jnp.concatenate(rows + [jnp.zeros((count - 4, wide), F32)], axis=0)


def tail_gain(piece, first):
    tail = piece[first : first + 16].astype(F32)
    return jnp.concatenate([tail[0:1] + tail[1:2], tail[2:3] + tail[3:4]], axis=1)


def between_a(*refs):
    kept_0, got_0, kept_1, got_1, gain = refs[0], refs[1:4], refs[4], refs[5:8], refs[8]
    kept, sends, gain_out = refs[9], refs[10:13], refs[13]
    rows = kept_0.shape[0]
    half = rows // 2
    first = added(kept_0, got_0)
    second = added(kept_1, got_1, slice(0, rows))
    gains = [tail_gain(piece, rows) for piece in got_1]
    total = (gain[...] + gains[0]) + (gains[1] + gains[2])
    gain_out[...] = total
    tail = tail_rows(total, 16)
    kept[...] = first[:half]
    for send, piece in zip(sends, (first[half:], second[:half], second[half:])):
        send[...] = jnp.concatenate([piece, tail], axis=0).astype(BF16)


def between_b(*refs):
    total = added(refs[0], refs[1:4])
    half = total.shape[0] // 2
    for s in range(4):
        piece = jnp.concatenate(
            [total[n * half + 16 * s : n * half + 16 * s + 16] for n in range(2)], axis=0
        )
        refs[4 + s][...] = piece.astype(refs[4 + s].dtype)


def before_z(*refs):
    kept_a, got_a, kept_b, got_b, gain = refs[0], refs[1:4], refs[4], refs[5:8], refs[8]
    kept, sends, gain_out = refs[9], refs[10:13], refs[13]
    rows = kept_a.shape[0]
    unit = rows // 4
    total = jnp.concatenate(
        [added(kept_a, got_a, slice(0, rows)), added(kept_b, got_b)], axis=1
    )
    gains = [tail_gain(piece, rows) for piece in got_a]
    share = (gain[...] + gains[0]) + (gains[1] + gains[2])
    gain_out[...] = share
    high = share.astype(BF16).astype(F32)
    tail = jnp.concatenate(
        [high, share - high, jnp.zeros((14 - unit, share.shape[1]), F32)], axis=0
    )
    kept[...] = total[:unit]
    for send, n in zip(sends, (2, 1, 3)):
        piece = total[n * unit : (n + 1) * unit]
        send[...] = jnp.concatenate([piece, tail], axis=0).astype(BF16)


def last_gain(kept, first, second, third, out):
    unit = first.shape[0] // 2
    tails = [piece[...].astype(F32)[unit:] for piece in (first, second, third)]
    shares = [tail[0:1] + tail[1:2] for tail in tails]
    out[...] = (kept[...] + shares[0]) + (shares[1] + shares[2])


def last_states(kept, first, second, third, states, gain, out):
    unit = kept.shape[0]
    pieces = [piece[...].astype(F32)[:unit] for piece in (first, second, third)]
    total = (kept[...] + pieces[0]) + (pieces[1] + pieces[2])
    own = states[...]
    inverse = lax.rsqrt(jnp.mean(own * own, axis=1, keepdims=True) + EPSILON)
    scaled = total * gain[...]
    out[...] = inverse * scaled - own * (inverse * inverse * inverse) * jnp.mean(
        own * scaled, axis=1, keepdims=True
    )


def body(hidden_states, final_gain, student_head, teacher_states, teacher_head, token_weight):
    y, zl, x, zh, c = (lax.axis_index(name) for name in AXES)
    z = zh * 2 + zl
    sign = 1 - 2 * c
    tokens = token_weight.shape[0]
    dt, ds = teacher_states.shape[1], hidden_states.shape[1]
    rows = hidden_states.shape[0] // 2
    unit = rows // 8
    half = tokens // 4

    def swap(array):
        return permute(array, lambda y, z, x, c: (y, z, x, 1 - c))

    kx, kz, i = row_parts(rows, 4, 2, unit)
    source = (((x + sign * kx) % 4 * 2 + (zh ^ kz)) * 2 + c) * unit + i
    select = pick(source, 2 * rows).astype(BF16)
    own = jnp.concatenate(
        [
            jnp.dot(select, states, preferred_element_type=F32).astype(BF16)
            for states in (teacher_states, hidden_states)
        ],
        axis=1,
    )
    teacher_other = swap(teacher_head)
    student_other = swap(student_head)

    from_y = moved(("y", "y"), -1)
    from_z = moved(("z", "z"), -1)
    own_states = own[:unit, dt:].astype(F32)
    y1, z0, own_states = lax.optimization_barrier(
        (permute(own, from_y), permute(own, from_z), own_states)
    )
    y2, z1 = lax.optimization_barrier((permute(y1, from_y), permute(y1, from_z)))
    gain_row = final_gain[None]
    y3, z2 = permute(y2, from_y), permute(y2, from_z)
    heads = (teacher_head, student_head, teacher_other, student_other)
    half_0 = logits_streamed([own, z0, y1, z1], gain_row, *heads)
    y3, z2, half_0, heads = lax.optimization_barrier((y3, z2, half_0, heads))
    z3_t, z3_h = permute(y3[:, :dt], from_z), permute(z2[:, dt:], from_y)
    student_heads = resident(heads[1], heads[3])
    z3_t, z3_h, student_heads = lax.optimization_barrier((z3_t, z3_h, student_heads))
    half_1 = logits(
        [y2, z2, y3, z3_t, z3_h],
        gain_row,
        *(heads[0], student_heads[0], heads[2], student_heads[1]),
    )

    ry, rb, kx, kz, i = row_parts(2 * half, 4, 2, 4, 2, unit)
    rz = kz * 2 + rb
    to_y, to_z, to_x = (y + sign * ry) % 4, (z + sign * rz) % 4, (x + sign * kx) % 4
    absolute = (((to_y * 2 + to_z % 2) * 4 + to_x) * 2 + to_z // 2) * unit + i
    order = pick(absolute, 2 * half).astype(F32)
    token = (absolute // unit * 2 + c) * unit + i
    weight = jnp.sum(jnp.where(pick(token, tokens), token_weight[None, :], 0.0), axis=1)

    local = jnp.concatenate([half_0[2][:2], half_1[2][:2]], axis=1)
    whole = jnp.dot(local, order, precision=lax.Precision.HIGHEST)
    spread = jnp.broadcast_to(whole.reshape(1, 8, -1), (64, 8, half // 2))
    every = lax.all_to_all(spread, AXES[:4], 0, 0, tiled=True)
    top = jnp.max(every, axis=0)
    whole = (top + jnp.log(jnp.sum(jnp.exp(every - top), axis=0))).reshape(whole.shape)
    relative = jnp.dot(whole, order.T, precision=lax.Precision.HIGHEST)
    rows = jnp.concatenate([relative, weight[None], jnp.zeros((5, 2 * half), F32)], axis=0)

    def exchange(pieces, axis):
        moves = {s: permute(pieces[s - 1], moved((axis, axis), s)) for s in (1, 3, 2)}
        return [moves[s] for s in (1, 2, 3)]

    head_pair = student_heads
    sends_0, kept_0, kept_b, send_b1, gain_0 = backward(
        half_0, rows[:, :half], gain_row, *head_pair
    )
    got_0 = exchange(sends_0, "x")
    got_b1 = permute(send_b1, moved(("y", "y"), 1))
    sends_1, kept_1, send_b2, send_b3, gain = backward(
        half_1, rows[:, half:], gain_row, *head_pair, gain_0
    )
    got_0, got_b1, sends_1, send_b2, send_b3 = lax.optimization_barrier(
        (got_0, got_b1, sends_1, send_b2, send_b3)
    )
    got_1 = exchange(sends_1, "x")
    got_b3 = permute(send_b3, moved(("y", "y"), 3))
    got_b2 = permute(send_b2, moved(("y", "y"), 2))
    wide = ds // 2
    count = half // 8
    kept_a, *sends_a, gain = small(
        between_a,
        [((count, wide), F32)] + [((count + 16, wide), BF16)] * 3 + [((1, ds), F32)],
        *(kept_0, *got_0, kept_1, *got_1, gain),
    )
    got_a = exchange(sends_a, "y")
    kept_b, *sends_b = small(
        between_b,
        [((count, wide), F32)] + [((count, wide), BF16)] * 3,
        *(kept_b, got_b1, got_b2, got_b3),
    )
    got_b = exchange(sends_b, "x")
    kept, *sends, gain = small(
        before_z,
        [((unit, ds), F32)] + [((16, ds), BF16)] * 3 + [((1, ds), F32)],
        *(kept_a, *got_a, kept_b, *got_b, gain),
    )
    got = exchange(sends, "z")
    (gain,) = small(last_gain, [((1, ds), F32)], gain, *got)
    gain_grad = (gain + swap(gain))[0]
    (states_grad,) = small(
        last_states, [((unit, ds), F32)], kept, *got, own_states, gain_row
    )
    return (states_grad, gain_grad)


def solution(mesh):
    torus = Mesh(mesh.devices.reshape(SIZES), AXES)
    return jax.shard_map(
        body,
        mesh=torus,
        in_specs=(
            P(("y", "zl"), None),
            P(),
            P(AXES, None),
            P(("y", "zl"), None),
            P(AXES, None),
            P(),
        ),
        out_specs=(P(AXES, None), P()),
        check_vma=False,
    )
```

```python
import functools

import jax
import jax.numpy as jnp
from jax import lax
from jax.experimental import pallas as pl
from jax.experimental.pallas import tpu as pltpu
from jax.sharding import Mesh, PartitionSpec as P

EPSILON = 1e-06
AXES = ("y", "zl", "x", "zh", "c")
SIZES = (4, 2, 4, 2, 2)
F32 = jnp.float32
BF16 = jnp.bfloat16
STREAMED = 58 * 2**20
LARGE = 30 * 2**20
SMALL = 3 * 2**20
GAIN = (32, 128)


def place(y, z, x, c):
    y, z, x, c = y % 4, z % 4, x % 4, c % 2
    return (((y * 2 + z % 2) * 4 + x) * 2 + z // 2) * 2 + c


def permute(array, target):
    pairs = [
        (place(y, z, x, c), place(*target(y, z, x, c)))
        for y in range(4)
        for z in range(4)
        for x in range(4)
        for c in range(2)
    ]
    return lax.ppermute(array, AXES, pairs)


def moved(axis, steps):
    def target(y, z, x, c):
        by = steps if c == 0 else -steps
        name = axis[c]
        return (y + by * (name == "y"), z + by * (name == "z"), x + by * (name == "x"), c)

    return target


def pick(rows, columns):
    return rows[:, None] == lax.broadcasted_iota(jnp.int32, (rows.shape[0], columns), 1)


def row_parts(count, *sizes):
    index = lax.iota(jnp.int32, count)
    digits = []
    for size in reversed(sizes):
        digits.append(index % size)
        index = index // size
    return digits[::-1]


def log_sum(parts):
    top = jnp.maximum(jnp.maximum(parts[0], parts[1]), jnp.maximum(parts[2], parts[3]))
    return top + jnp.log(sum(jnp.exp(part - top) for part in parts))


def columns_to_rows(columns):
    rows = columns[0].shape[0]
    wide = jnp.concatenate(
        columns + [jnp.zeros((rows, 128 - len(columns)), F32)], axis=1
    )
    return wide.T[:8]


def rows_to_columns(rows):
    count = rows.shape[1]
    return jnp.concatenate([rows, jnp.zeros((120, count), F32)], axis=0).T


def resident_kernel(*refs):
    count = (len(refs) - 1) // 2
    sem = refs[-1]
    copies = [
        pltpu.make_async_copy(refs[n], refs[count + n], sem.at[n]) for n in range(count)
    ]
    for copy in copies:
        copy.start()
    for copy in copies:
        copy.wait()


def resident(*arrays):
    return pl.pallas_call(
        resident_kernel,
        in_specs=[pl.BlockSpec(memory_space=pl.ANY)] * len(arrays),
        out_specs=[pl.BlockSpec(memory_space=pltpu.VMEM)] * len(arrays),
        out_shape=[pltpu.VMEM(array.shape, array.dtype) for array in arrays],
        scratch_shapes=[pltpu.SemaphoreType.DMA((len(arrays),))],
        compiler_params=pltpu.CompilerParams(vmem_limit_bytes=SMALL),
        cost_estimate=pl.CostEstimate(
            flops=0, bytes_accessed=4 * sum(a.size for a in arrays), transcendentals=0
        ),
    )(*[pltpu.with_memory_space_constraint(array, pltpu.HBM) for array in arrays])


def logits_kernel(tile, *refs):
    blocks, refs = refs[:-12], refs[-12:]
    gain, own_t, own_s, other_t, other_s, out_t, out_s, lse, normed, states_t, wait, sem = refs
    rows, vocab, dt = blocks[0].shape[0], own_t.shape[0], own_t.shape[1]
    slots = wait.shape[0]
    copies = [
        pltpu.make_async_copy(
            head.at[pl.ds(first, tile)], wait.at[n % slots], sem.at[n % slots]
        )
        for n, (head, first) in enumerate(
            (head, first) for head in (own_t, other_t) for first in range(0, vocab, tile)
        )
    ]
    for n in range(slots):
        copies[n].start()
    for k in range(4):
        span = pl.ds(k * rows, rows)
        block = blocks[k]
        states_t[span, :] = block[:, :dt]
        wide = (block[:, dt:] if block.shape[1] > dt else blocks[4][...]).astype(F32)
        inverse = lax.rsqrt(jnp.mean(wide * wide, axis=1, keepdims=True) + EPSILON)
        normed[span, :] = (wide * inverse * gain[...]).astype(BF16)
    count = states_t.shape[0]

    def statistics(out, n, top, total):
        part = out[:, pl.ds(n * tile, tile)]
        new = jnp.maximum(top, jnp.max(part, axis=1, keepdims=True))
        total = total * jnp.exp(top - new) + jnp.sum(
            jnp.exp(part - new), axis=1, keepdims=True
        )
        return new, total

    sums = []
    for states, out in ((normed, out_s), (states_t, out_t)):
        top = jnp.full((count, 1), -jnp.inf, F32)
        total = jnp.zeros((count, 1), F32)
        for n in range(2 * vocab // tile):
            if out is out_s:
                head = (own_s, other_s)[n * tile // vocab]
                head = head[pl.ds(n * tile % vocab, tile), :]
            else:
                copies[n].wait()
                head = wait[n % slots]
            out[:, pl.ds(n * tile, tile)] = lax.dot_general(
                states[...], head, (((1,), (1,)), ((), ())), preferred_element_type=F32
            )
            if out is out_t and n + slots < len(copies):
                copies[n + slots].start()
            if n:
                top, total = statistics(out, n - 1, top, total)
        top, total = statistics(out, 2 * vocab // tile - 1, top, total)
        sums.append(top + jnp.log(total))
    lse[...] = columns_to_rows(sums[::-1])


def streamed_kernel(tile, *refs):
    blocks, (gain, own_t, own_s, other_t, other_s) = refs[:4], refs[4:9]
    out_t, out_s, lse, normed, states_t, wait_t, wait_s, sem = refs[9:]
    rows, dt, vocab = blocks[0].shape[0], states_t.shape[1], own_t.shape[0]
    slots = wait_t.shape[0]
    work = []
    for pair, base in (((own_t, own_s), 0), ((other_t, other_s), vocab)):
        for kind in range(2):
            for first in range(0, vocab, tile):
                work.append((kind, pair[kind], first, base + first))
    copies, slot, used = [], [], [0, 0]
    for kind, head, first, _ in work:
        slot.append(used[kind] % slots)
        used[kind] += 1
        copies.append(
            pltpu.make_async_copy(
                head.at[pl.ds(first, tile)],
                (wait_t, wait_s)[kind].at[slot[-1]],
                sem.at[kind, slot[-1]],
            )
        )
    ahead = slots - 1
    for k in range(ahead):
        copies[k].start()
    for k, block in enumerate(blocks):
        span = pl.ds(k * rows, rows)
        states_t[span, :] = block[:, :dt]
        wide = block[:, dt:].astype(F32)
        inverse = lax.rsqrt(jnp.mean(wide * wide, axis=1, keepdims=True) + EPSILON)
        normed[span, :] = (wide * inverse * gain[...]).astype(BF16)
    count = states_t.shape[0]
    top = [jnp.full((count, 1), -jnp.inf, F32)] * 2
    total = [jnp.zeros((count, 1), F32)] * 2
    outs = (out_t, out_s)

    def statistics(k):
        kind, _, _, base = work[k]
        part = outs[kind][:, pl.ds(base, tile)]
        new = jnp.maximum(top[kind], jnp.max(part, axis=1, keepdims=True))
        total[kind] = total[kind] * jnp.exp(top[kind] - new) + jnp.sum(
            jnp.exp(part - new), axis=1, keepdims=True
        )
        top[kind] = new

    for k, (kind, _, _, base) in enumerate(work):
        copies[k].wait()
        if k + ahead < len(work):
            copies[k + ahead].start()
        outs[kind][:, pl.ds(base, tile)] = lax.dot_general(
            (states_t, normed)[kind][...],
            (wait_t, wait_s)[kind][slot[k]],
            (((1,), (1,)), ((), ())),
            preferred_element_type=F32,
        )
        if k:
            statistics(k - 1)
    statistics(len(work) - 1)
    lse[...] = columns_to_rows([t + jnp.log(z) for t, z in zip(top, total)])


def logits_streamed(blocks, gain, own_t, own_s, other_t, other_s):
    count = 4 * blocks[0].shape[0]
    vocab, dt = own_t.shape
    ds = own_s.shape[1]
    tile, slots = 512, 3
    vmem = pl.BlockSpec(memory_space=pltpu.VMEM)
    anywhere = pl.BlockSpec(memory_space=pl.ANY)
    return pl.pallas_call(
        functools.partial(streamed_kernel, tile),
        in_specs=[vmem] * 5 + [anywhere] * 4,
        out_specs=[vmem] * 4,
        out_shape=[
            jax.ShapeDtypeStruct((count, 2 * vocab), F32),
            jax.ShapeDtypeStruct((count, 2 * vocab), F32),
            jax.ShapeDtypeStruct((8, count), F32),
            jax.ShapeDtypeStruct((count, ds), BF16),
        ],
        scratch_shapes=[
            pltpu.VMEM((count, dt), BF16),
            pltpu.VMEM((slots, tile, dt), BF16),
            pltpu.VMEM((slots, tile, ds), BF16),
            pltpu.SemaphoreType.DMA((2, slots)),
        ],
        compiler_params=pltpu.CompilerParams(vmem_limit_bytes=STREAMED),
        cost_estimate=pl.CostEstimate(
            flops=4 * count * vocab * (dt + ds),
            bytes_accessed=4 * vocab * (dt + ds),
            transcendentals=4 * vocab * count,
        ),
    )(*blocks, gain, own_t, own_s, other_t, other_s)


def held(array):
    return pltpu.with_memory_space_constraint(array, pltpu.VMEM)


def logits(blocks, gain, own_t, own_s, other_t, other_s):
    count = 4 * blocks[0].shape[0]
    vocab, dt = own_t.shape
    ds = own_s.shape[1]
    tile, slots = 512, 2
    vmem = pl.BlockSpec(memory_space=pltpu.VMEM)
    anywhere = pl.BlockSpec(memory_space=pl.ANY)
    return pl.pallas_call(
        functools.partial(logits_kernel, tile),
        in_specs=[vmem] * (len(blocks) + 1) + [anywhere, vmem] * 2,
        out_specs=[vmem] * 4,
        out_shape=[
            jax.ShapeDtypeStruct((count, 2 * vocab), F32),
            jax.ShapeDtypeStruct((count, 2 * vocab), F32),
            jax.ShapeDtypeStruct((8, count), F32),
            jax.ShapeDtypeStruct((count, ds), BF16),
        ],
        scratch_shapes=[
            pltpu.VMEM((count, dt), BF16),
            pltpu.VMEM((slots, tile, dt), BF16),
            pltpu.SemaphoreType.DMA((slots,)),
        ],
        compiler_params=pltpu.CompilerParams(vmem_limit_bytes=LARGE),
        cost_estimate=pl.CostEstimate(
            flops=4 * count * vocab * (dt + ds),
            bytes_accessed=4 * vocab * (dt + ds),
            transcendentals=4 * vocab * count,
        ),
    )(*blocks, gain, own_t, held(own_s), other_t, held(other_s))


def backward_kernel(tile, later, *refs):
    teacher, student, normed, rows, gain, own, other = refs[:7]
    before = refs[7] if later else None
    refs = refs[7 + later :]
    sends_a, kept_a, refs = refs[:3], refs[3], refs[4:]
    outs_b, (gain_out, grad) = refs[:2], refs[2:]
    half, vocab = teacher.shape
    part, ds = own.shape
    steps = ds // tile
    columns = rows_to_columns(rows[...])
    lse_t, lse_s, weight = (columns[:, k : k + 1] for k in range(3))
    for first in range(0, vocab, 512):
        at = pl.ds(first, 512)
        gap = jnp.exp(student[:, at] - lse_s) - jnp.exp(teacher[:, at] - lse_t)
        grad[:, at] = (weight * gap).astype(BF16)
    for k in range(steps):
        at = pl.ds(k * tile, tile)
        out = jnp.dot(grad[:, :part], own[:, at], preferred_element_type=F32)
        out += jnp.dot(grad[:, part:], other[:, at], preferred_element_type=F32)
        share = jnp.sum(out * normed[:, at].astype(F32), axis=0, keepdims=True)
        share /= gain[:, at]
        for n in range(tile // 128):
            row = pl.ds(k * tile // 128 + n, 1)
            piece = share[:, 128 * n : 128 * (n + 1)]
            gain_out[row, :] = piece + before[row, :] if later else piece
        second = k >= steps // 2
        at = pl.ds((k - second * (steps // 2)) * tile, tile)
        if second:
            for n in range(2):
                outs_b[n][:, at] = out[n * half // 2 : (n + 1) * half // 2].astype(
                    outs_b[n].dtype
                )
        else:
            for s in range(4):
                groups = [
                    out[64 * j + 16 * s : 64 * j + 16 * s + 16] for j in range(half // 64)
                ]
                piece = jnp.concatenate(groups, axis=0)
                if s == 0:
                    kept_a[:, at] = piece
                else:
                    sends_a[s - 1][:, at] = piece.astype(BF16)
    used = ds // 128
    gain_out[used:, :] = jnp.zeros((gain_out.shape[0] - used, 128), F32)
    if later:
        tail = packed(gain_out[...], half // 4).astype(BF16)
        for send in sends_a:
            send[:, pl.ds(ds // 2, 128)] = tail


def packed(gain, rows):
    high = gain.astype(BF16).astype(F32)
    parts = jnp.concatenate([high, gain - high], axis=0)
    count = parts.shape[0]
    return jnp.concatenate(
        [parts[first : first + rows] for first in range(0, count, rows)], axis=1
    )


def unpacked(tail):
    tail = tail.astype(F32)
    parts = jnp.concatenate(
        [tail[:, first : first + 128] for first in range(0, tail.shape[1], 128)], axis=0
    )
    half = parts.shape[0] // 2
    return parts[:half] + parts[half:]


def backward(part_of, rows, gain, own, other, before=None):
    teacher, student, _, normed = part_of
    later = before is not None
    half, vocab = teacher.shape
    part, ds = own.shape
    tile = ds // 4
    count = half // 4
    vmem = pl.BlockSpec(memory_space=pltpu.VMEM)
    wide = ds // 2
    out = pl.pallas_call(
        functools.partial(backward_kernel, tile, later),
        in_specs=[vmem] * (7 + later),
        out_specs=[vmem] * 7,
        out_shape=[jax.ShapeDtypeStruct((count, wide + 128 * later), BF16)] * 3
        + [jax.ShapeDtypeStruct((count, wide), F32)]
        + [jax.ShapeDtypeStruct((2 * count, wide), BF16 if later else F32)]
        + [jax.ShapeDtypeStruct((2 * count, wide), BF16)]
        + [jax.ShapeDtypeStruct(GAIN, F32)],
        scratch_shapes=[pltpu.VMEM((half, vocab), BF16)],
        compiler_params=pltpu.CompilerParams(vmem_limit_bytes=SMALL),
        cost_estimate=pl.CostEstimate(
            flops=2 * half * vocab * ds,
            bytes_accessed=2 * vocab * ds,
            transcendentals=2 * vocab * half,
        ),
    )(teacher, student, normed, rows, gain, held(own), held(other), *([before] if later else []))
    return out[:3], out[3], out[4], out[5], out[6]


def small(kernel, out_shape, *args):
    vmem = pl.BlockSpec(memory_space=pltpu.VMEM)
    return pl.pallas_call(
        kernel,
        in_specs=[vmem] * len(args),
        out_specs=[vmem] * len(out_shape),
        out_shape=[jax.ShapeDtypeStruct(*shape) for shape in out_shape],
        compiler_params=pltpu.CompilerParams(vmem_limit_bytes=SMALL),
    )(*args)


def added(kept, pieces):
    wide = kept.shape[1]
    first, second, third = (piece[:, :wide].astype(F32) for piece in pieces)
    return (kept[...] + first) + (second + third)


def added_gain(gain, pieces, wide):
    first, second, third = (unpacked(piece[:, wide:]) for piece in pieces)
    return (gain[...] + first) + (second + third)


def between_a(*refs):
    kept_0, got_0, kept_1, got_1, gain = refs[0], refs[1:4], refs[4], refs[5:8], refs[8]
    kept, sends, gain_out = refs[9], refs[10:13], refs[13]
    half = kept_0.shape[0] // 2
    first = added(kept_0, got_0)
    second = added(kept_1, got_1)
    total = added_gain(gain, got_1, kept_0.shape[1])
    gain_out[...] = total
    tail = packed(total, half)
    kept[...] = first[:half]
    for send, piece in zip(sends, (first[half:], second[:half], second[half:])):
        send[...] = jnp.concatenate([piece, tail], axis=1).astype(BF16)


def between_b(*refs):
    total = added(refs[0], refs[1:4])
    half = total.shape[0] // 2
    for s in range(4):
        piece = jnp.concatenate(
            [total[n * half + 16 * s : n * half + 16 * s + 16] for n in range(2)], axis=0
        )
        refs[4 + s][...] = piece.astype(refs[4 + s].dtype)


def before_z(*refs):
    kept_a, got_a, kept_b, got_b, gain = refs[0], refs[1:4], refs[4], refs[5:8], refs[8]
    kept, sends, gain_out = refs[9], refs[10:13], refs[13]
    rows, wide = kept_a.shape
    unit = rows // 4
    total = jnp.concatenate([added(kept_a, got_a), added(kept_b, got_b)], axis=1)
    share = added_gain(gain, got_a, wide)
    gain_out[...] = share
    tail = packed(share, unit)
    kept[...] = total[:unit]
    for send, n in zip(sends, (2, 1, 3)):
        piece = total[n * unit : (n + 1) * unit]
        send[...] = jnp.concatenate([piece, tail], axis=1).astype(BF16)


def last_gain(gain, first, second, third, out):
    wide = first.shape[1] - 2 * gain.size // first.shape[0]
    out[...] = added_gain(gain, (first, second, third), wide)


def last_states(kept, first, second, third, states, gain, out):
    total = added(kept, (first, second, third))
    own = states[...]
    inverse = lax.rsqrt(jnp.mean(own * own, axis=1, keepdims=True) + EPSILON)
    scaled = total * gain[...]
    out[...] = inverse * scaled - own * (inverse * inverse * inverse) * jnp.mean(
        own * scaled, axis=1, keepdims=True
    )


def body(hidden_states, final_gain, student_head, teacher_states, teacher_head, token_weight):
    y, zl, x, zh, c = (lax.axis_index(name) for name in AXES)
    z = zh * 2 + zl
    sign = 1 - 2 * c
    tokens = token_weight.shape[0]
    dt, ds = teacher_states.shape[1], hidden_states.shape[1]
    rows = hidden_states.shape[0] // 2
    unit = rows // 8
    half = tokens // 4

    def swap(array):
        return permute(array, lambda y, z, x, c: (y, z, x, 1 - c))

    kx, kz, i = row_parts(rows, 4, 2, unit)
    source = (((x + sign * kx) % 4 * 2 + (zh ^ kz)) * 2 + c) * unit + i
    select = pick(source, 2 * rows).astype(BF16)
    own = jnp.concatenate(
        [
            jnp.dot(select, states, preferred_element_type=F32).astype(BF16)
            for states in (teacher_states, hidden_states)
        ],
        axis=1,
    )
    teacher_other = swap(teacher_head)
    student_other = swap(student_head)

    from_y = moved(("y", "y"), -1)
    from_z = moved(("z", "z"), -1)
    own_states = own[:unit, dt:].astype(F32)
    y1, z0, own_states = lax.optimization_barrier(
        (permute(own, from_y), permute(own, from_z), own_states)
    )
    y2, z1 = lax.optimization_barrier((permute(y1, from_y), permute(y1, from_z)))
    gain_row = final_gain[None]
    y3, z2 = permute(y2, from_y), permute(y2, from_z)
    heads = (teacher_head, student_head, teacher_other, student_other)
    half_0 = logits_streamed([own, z0, y1, z1], gain_row, *heads)
    y3, z2, half_0, heads = lax.optimization_barrier((y3, z2, half_0, heads))
    z3_t, z3_h = permute(y3[:, :dt], from_z), permute(z2[:, dt:], from_y)
    student_heads = resident(heads[1], heads[3])
    z3_t, z3_h, student_heads = lax.optimization_barrier((z3_t, z3_h, student_heads))
    half_1 = logits(
        [y2, z2, y3, z3_t, z3_h],
        gain_row,
        *(heads[0], student_heads[0], heads[2], student_heads[1]),
    )

    ry, rb, kx, kz, i = row_parts(2 * half, 4, 2, 4, 2, unit)
    rz = kz * 2 + rb
    to_y, to_z, to_x = (y + sign * ry) % 4, (z + sign * rz) % 4, (x + sign * kx) % 4
    absolute = (((to_y * 2 + to_z % 2) * 4 + to_x) * 2 + to_z // 2) * unit + i
    order = pick(absolute, 2 * half).astype(F32)
    token = (absolute // unit * 2 + c) * unit + i
    weight = jnp.sum(jnp.where(pick(token, tokens), token_weight[None, :], 0.0), axis=1)

    local = jnp.concatenate([half_0[2][:2], half_1[2][:2]], axis=1)
    whole = jnp.dot(local, order, precision=lax.Precision.HIGHEST)
    for axis in ("x", "y", "z"):
        parts = [whole] + [permute(whole, moved((axis, axis), s)) for s in (1, 3, 2)]
        whole = log_sum(parts)
    relative = jnp.dot(whole, order.T, precision=lax.Precision.HIGHEST)
    rows = jnp.concatenate([relative, weight[None], jnp.zeros((5, 2 * half), F32)], axis=0)

    def exchange(pieces, axis):
        moves = {s: permute(pieces[s - 1], moved((axis, axis), s)) for s in (1, 3, 2)}
        return [moves[s] for s in (1, 2, 3)]

    head_pair = student_heads
    sends_0, kept_0, kept_b, send_b1, gain_0 = backward(
        half_0, rows[:, :half], gain_row, *head_pair
    )
    got_0 = exchange(sends_0, "x")
    got_b1 = permute(send_b1, moved(("y", "y"), 1))
    sends_1, kept_1, send_b2, send_b3, gain = backward(
        half_1, rows[:, half:], gain_row, *head_pair, gain_0
    )
    got_0, got_b1, sends_1, send_b2, send_b3 = lax.optimization_barrier(
        (got_0, got_b1, sends_1, send_b2, send_b3)
    )
    got_1 = exchange(sends_1, "x")
    got_b3 = permute(send_b3, moved(("y", "y"), 3))
    got_b2 = permute(send_b2, moved(("y", "y"), 2))
    wide = ds // 2
    count = half // 8
    kept_a, *sends_a, gain = small(
        between_a,
        [((count, wide), F32)] + [((count, wide + 256), BF16)] * 3 + [(GAIN, F32)],
        *(kept_0, *got_0, kept_1, *got_1, gain),
    )
    got_a = exchange(sends_a, "y")
    kept_b, *sends_b = small(
        between_b,
        [((count, wide), F32)] + [((count, wide), BF16)] * 3,
        *(kept_b, got_b1, got_b2, got_b3),
    )
    got_b = exchange(sends_b, "x")
    kept, *sends, gain = small(
        before_z,
        [((unit, ds), F32)] + [((unit, ds + 1024), BF16)] * 3 + [(GAIN, F32)],
        *(kept_a, *got_a, kept_b, *got_b, gain),
    )
    got = exchange(sends, "z")
    (gain,) = small(last_gain, [(GAIN, F32)], gain, *got)
    gain_grad = (gain + swap(gain)).reshape(-1)[:ds]
    (states_grad,) = small(
        last_states, [((unit, ds), F32)], kept, *got, own_states, gain_row
    )
    return (states_grad, gain_grad)


def solution(mesh):
    torus = Mesh(mesh.devices.reshape(SIZES), AXES)
    return jax.shard_map(
        body,
        mesh=torus,
        in_specs=(
            P(("y", "zl"), None),
            P(),
            P(AXES, None),
            P(("y", "zl"), None),
            P(AXES, None),
            P(),
        ),
        out_specs=(P(AXES, None), P()),
        check_vma=False,
    )
```

```python
import functools

import jax
import jax.numpy as jnp
from jax import lax
from jax.experimental import pallas as pl
from jax.experimental.pallas import tpu as pltpu
from jax.sharding import Mesh, PartitionSpec as P

EPSILON = 1e-06
AXES = ("y", "zl", "x", "zh", "c")
SIZES = (4, 2, 4, 2, 2)
F32 = jnp.float32
BF16 = jnp.bfloat16
LARGE = 26 * 2**20
SMALL = 3 * 2**20
GAIN = (32, 128)


def place(y, z, x, c):
    y, z, x, c = y % 4, z % 4, x % 4, c % 2
    return (((y * 2 + z % 2) * 4 + x) * 2 + z // 2) * 2 + c


def permute(array, target):
    pairs = [
        (place(y, z, x, c), place(*target(y, z, x, c)))
        for y in range(4)
        for z in range(4)
        for x in range(4)
        for c in range(2)
    ]
    return lax.ppermute(array, AXES, pairs)


def moved(axis, steps):
    def target(y, z, x, c):
        by = steps if c == 0 else -steps
        name = axis[c]
        return (y + by * (name == "y"), z + by * (name == "z"), x + by * (name == "x"), c)

    return target


def pick(rows, columns):
    return rows[:, None] == lax.broadcasted_iota(jnp.int32, (rows.shape[0], columns), 1)


def row_parts(count, *sizes):
    index = lax.iota(jnp.int32, count)
    digits = []
    for size in reversed(sizes):
        digits.append(index % size)
        index = index // size
    return digits[::-1]


def log_sum(parts):
    top = jnp.maximum(jnp.maximum(parts[0], parts[1]), jnp.maximum(parts[2], parts[3]))
    return top + jnp.log(sum(jnp.exp(part - top) for part in parts))


def columns_to_rows(columns):
    rows = columns[0].shape[0]
    wide = jnp.concatenate(
        columns + [jnp.zeros((rows, 128 - len(columns)), F32)], axis=1
    )
    return wide.T[:8]


def rows_to_columns(rows):
    count = rows.shape[1]
    return jnp.concatenate([rows, jnp.zeros((120, count), F32)], axis=0).T


def resident_kernel(*refs):
    count = (len(refs) - 1) // 2
    sem = refs[-1]
    copies = [
        pltpu.make_async_copy(refs[n], refs[count + n], sem.at[n]) for n in range(count)
    ]
    for copy in copies:
        copy.start()
    for copy in copies:
        copy.wait()


def resident(*arrays):
    return pl.pallas_call(
        resident_kernel,
        in_specs=[pl.BlockSpec(memory_space=pl.ANY)] * len(arrays),
        out_specs=[pl.BlockSpec(memory_space=pltpu.VMEM)] * len(arrays),
        out_shape=[pltpu.VMEM(array.shape, array.dtype) for array in arrays],
        scratch_shapes=[pltpu.SemaphoreType.DMA((len(arrays),))],
        compiler_params=pltpu.CompilerParams(vmem_limit_bytes=SMALL),
        cost_estimate=pl.CostEstimate(
            flops=0, bytes_accessed=4 * sum(a.size for a in arrays), transcendentals=0
        ),
    )(*[pltpu.with_memory_space_constraint(array, pltpu.HBM) for array in arrays])


def logits_kernel(tile, *refs):
    blocks, refs = refs[:-12], refs[-12:]
    gain, own_t, own_s, other_t, other_s, out_t, out_s, lse, normed, states_t, wait, sem = refs
    rows, vocab, dt = blocks[0].shape[0], own_t.shape[0], own_t.shape[1]
    slots = wait.shape[0]
    copies = [
        pltpu.make_async_copy(
            head.at[pl.ds(first, tile)], wait.at[n % slots], sem.at[n % slots]
        )
        for n, (head, first) in enumerate(
            (head, first) for head in (own_t, other_t) for first in range(0, vocab, tile)
        )
    ]
    for n in range(slots):
        copies[n].start()
    for k in range(4):
        span = pl.ds(k * rows, rows)
        block = blocks[k]
        states_t[span, :] = block[:, :dt]
        wide = (block[:, dt:] if block.shape[1] > dt else blocks[4][...]).astype(F32)
        inverse = lax.rsqrt(jnp.mean(wide * wide, axis=1, keepdims=True) + EPSILON)
        normed[span, :] = (wide * inverse * gain[...]).astype(BF16)
    count = states_t.shape[0]

    def statistics(out, n, top, total):
        part = out[:, pl.ds(n * tile, tile)]
        new = jnp.maximum(top, jnp.max(part, axis=1, keepdims=True))
        total = total * jnp.exp(top - new) + jnp.sum(
            jnp.exp(part - new), axis=1, keepdims=True
        )
        return new, total

    sums = []
    for states, out in ((normed, out_s), (states_t, out_t)):
        top = jnp.full((count, 1), -jnp.inf, F32)
        total = jnp.zeros((count, 1), F32)
        for n in range(2 * vocab // tile):
            if out is out_s:
                head = (own_s, other_s)[n * tile // vocab]
                head = head[pl.ds(n * tile % vocab, tile), :]
            else:
                copies[n].wait()
                head = wait[n % slots]
            out[:, pl.ds(n * tile, tile)] = lax.dot_general(
                states[...], head, (((1,), (1,)), ((), ())), preferred_element_type=F32
            )
            if out is out_t and n + slots < len(copies):
                copies[n + slots].start()
            if n:
                top, total = statistics(out, n - 1, top, total)
        top, total = statistics(out, 2 * vocab // tile - 1, top, total)
        sums.append(top + jnp.log(total))
    lse[...] = columns_to_rows(sums[::-1])


def held(array):
    return pltpu.with_memory_space_constraint(array, pltpu.VMEM)


def logits(blocks, gain, own_t, own_s, other_t, other_s):
    count = 4 * blocks[0].shape[0]
    vocab, dt = own_t.shape
    ds = own_s.shape[1]
    tile, slots = 512, 2
    vmem = pl.BlockSpec(memory_space=pltpu.VMEM)
    anywhere = pl.BlockSpec(memory_space=pl.ANY)
    return pl.pallas_call(
        functools.partial(logits_kernel, tile),
        in_specs=[vmem] * (len(blocks) + 1) + [anywhere, vmem] * 2,
        out_specs=[vmem] * 4,
        out_shape=[
            jax.ShapeDtypeStruct((count, 2 * vocab), F32),
            jax.ShapeDtypeStruct((count, 2 * vocab), F32),
            jax.ShapeDtypeStruct((8, count), F32),
            jax.ShapeDtypeStruct((count, ds), BF16),
        ],
        scratch_shapes=[
            pltpu.VMEM((count, dt), BF16),
            pltpu.VMEM((slots, tile, dt), BF16),
            pltpu.SemaphoreType.DMA((slots,)),
        ],
        compiler_params=pltpu.CompilerParams(vmem_limit_bytes=LARGE),
        cost_estimate=pl.CostEstimate(
            flops=4 * count * vocab * (dt + ds),
            bytes_accessed=4 * vocab * (dt + ds),
            transcendentals=4 * vocab * count,
        ),
    )(*blocks, gain, own_t, held(own_s), other_t, held(other_s))


def backward_kernel(tile, later, *refs):
    teacher, student, normed, rows, gain, own, other = refs[:7]
    before = refs[7] if later else None
    refs = refs[7 + later :]
    sends_a, kept_a, refs = refs[:3], refs[3], refs[4:]
    outs_b, (gain_out, grad) = refs[:2], refs[2:]
    half, vocab = teacher.shape
    part, ds = own.shape
    steps = ds // tile
    columns = rows_to_columns(rows[...])
    lse_t, lse_s, weight = (columns[:, k : k + 1] for k in range(3))
    for first in range(0, vocab, 512):
        at = pl.ds(first, 512)
        gap = jnp.exp(student[:, at] - lse_s) - jnp.exp(teacher[:, at] - lse_t)
        grad[:, at] = (weight * gap).astype(BF16)
    for k in range(steps):
        at = pl.ds(k * tile, tile)
        out = jnp.dot(grad[:, :part], own[:, at], preferred_element_type=F32)
        out += jnp.dot(grad[:, part:], other[:, at], preferred_element_type=F32)
        share = jnp.sum(out * normed[:, at].astype(F32), axis=0, keepdims=True)
        share /= gain[:, at]
        for n in range(tile // 128):
            row = pl.ds(k * tile // 128 + n, 1)
            piece = share[:, 128 * n : 128 * (n + 1)]
            gain_out[row, :] = piece + before[row, :] if later else piece
        second = k >= steps // 2
        at = pl.ds((k - second * (steps // 2)) * tile, tile)
        if second:
            for n in range(2):
                outs_b[n][:, at] = out[n * half // 2 : (n + 1) * half // 2].astype(
                    outs_b[n].dtype
                )
        else:
            for s in range(4):
                groups = [
                    out[64 * j + 16 * s : 64 * j + 16 * s + 16] for j in range(half // 64)
                ]
                piece = jnp.concatenate(groups, axis=0)
                if s == 0:
                    kept_a[:, at] = piece
                else:
                    sends_a[s - 1][:, at] = piece.astype(BF16)
    used = ds // 128
    gain_out[used:, :] = jnp.zeros((gain_out.shape[0] - used, 128), F32)
    if later:
        tail = packed(gain_out[...], half // 4).astype(BF16)
        for send in sends_a:
            send[:, pl.ds(ds // 2, 128)] = tail


def packed(gain, rows):
    high = gain.astype(BF16).astype(F32)
    parts = jnp.concatenate([high, gain - high], axis=0)
    count = parts.shape[0]
    return jnp.concatenate(
        [parts[first : first + rows] for first in range(0, count, rows)], axis=1
    )


def unpacked(tail):
    tail = tail.astype(F32)
    parts = jnp.concatenate(
        [tail[:, first : first + 128] for first in range(0, tail.shape[1], 128)], axis=0
    )
    half = parts.shape[0] // 2
    return parts[:half] + parts[half:]


def backward(part_of, rows, gain, own, other, before=None):
    teacher, student, _, normed = part_of
    later = before is not None
    half, vocab = teacher.shape
    part, ds = own.shape
    tile = ds // 4
    count = half // 4
    vmem = pl.BlockSpec(memory_space=pltpu.VMEM)
    wide = ds // 2
    out = pl.pallas_call(
        functools.partial(backward_kernel, tile, later),
        in_specs=[vmem] * (7 + later),
        out_specs=[vmem] * 7,
        out_shape=[jax.ShapeDtypeStruct((count, wide + 128 * later), BF16)] * 3
        + [jax.ShapeDtypeStruct((count, wide), F32)]
        + [jax.ShapeDtypeStruct((2 * count, wide), BF16 if later else F32)]
        + [jax.ShapeDtypeStruct((2 * count, wide), BF16)]
        + [jax.ShapeDtypeStruct(GAIN, F32)],
        scratch_shapes=[pltpu.VMEM((half, vocab), BF16)],
        compiler_params=pltpu.CompilerParams(vmem_limit_bytes=SMALL),
        cost_estimate=pl.CostEstimate(
            flops=2 * half * vocab * ds,
            bytes_accessed=2 * vocab * ds,
            transcendentals=2 * vocab * half,
        ),
    )(teacher, student, normed, rows, gain, held(own), held(other), *([before] if later else []))
    return out[:3], out[3], out[4], out[5], out[6]


def small(kernel, out_shape, *args):
    vmem = pl.BlockSpec(memory_space=pltpu.VMEM)
    return pl.pallas_call(
        kernel,
        in_specs=[vmem] * len(args),
        out_specs=[vmem] * len(out_shape),
        out_shape=[jax.ShapeDtypeStruct(*shape) for shape in out_shape],
        compiler_params=pltpu.CompilerParams(vmem_limit_bytes=SMALL),
    )(*args)


def added(kept, pieces):
    wide = kept.shape[1]
    first, second, third = (piece[:, :wide].astype(F32) for piece in pieces)
    return (kept[...] + first) + (second + third)


def added_gain(gain, pieces, wide):
    first, second, third = (unpacked(piece[:, wide:]) for piece in pieces)
    return (gain[...] + first) + (second + third)


def between_a(*refs):
    kept_0, got_0, kept_1, got_1, gain = refs[0], refs[1:4], refs[4], refs[5:8], refs[8]
    kept, sends, gain_out = refs[9], refs[10:13], refs[13]
    half = kept_0.shape[0] // 2
    first = added(kept_0, got_0)
    second = added(kept_1, got_1)
    total = added_gain(gain, got_1, kept_0.shape[1])
    gain_out[...] = total
    tail = packed(total, half)
    kept[...] = first[:half]
    for send, piece in zip(sends, (first[half:], second[:half], second[half:])):
        send[...] = jnp.concatenate([piece, tail], axis=1).astype(BF16)


def between_b(*refs):
    total = added(refs[0], refs[1:4])
    half = total.shape[0] // 2
    for s in range(4):
        piece = jnp.concatenate(
            [total[n * half + 16 * s : n * half + 16 * s + 16] for n in range(2)], axis=0
        )
        refs[4 + s][...] = piece.astype(refs[4 + s].dtype)


def before_z(*refs):
    kept_a, got_a, kept_b, got_b, gain = refs[0], refs[1:4], refs[4], refs[5:8], refs[8]
    kept, sends, gain_out = refs[9], refs[10:13], refs[13]
    rows, wide = kept_a.shape
    unit = rows // 4
    total = jnp.concatenate([added(kept_a, got_a), added(kept_b, got_b)], axis=1)
    share = added_gain(gain, got_a, wide)
    gain_out[...] = share
    tail = packed(share, unit)
    kept[...] = total[:unit]
    for send, n in zip(sends, (2, 1, 3)):
        piece = total[n * unit : (n + 1) * unit]
        send[...] = jnp.concatenate([piece, tail], axis=1).astype(BF16)


def last_gain(gain, first, second, third, out):
    wide = first.shape[1] - 2 * gain.size // first.shape[0]
    out[...] = added_gain(gain, (first, second, third), wide)


def last_states(kept, first, second, third, states, gain, out):
    total = added(kept, (first, second, third))
    own = states[...]
    inverse = lax.rsqrt(jnp.mean(own * own, axis=1, keepdims=True) + EPSILON)
    scaled = total * gain[...]
    out[...] = inverse * scaled - own * (inverse * inverse * inverse) * jnp.mean(
        own * scaled, axis=1, keepdims=True
    )


def body(hidden_states, final_gain, student_head, teacher_states, teacher_head, token_weight):
    y, zl, x, zh, c = (lax.axis_index(name) for name in AXES)
    z = zh * 2 + zl
    sign = 1 - 2 * c
    tokens = token_weight.shape[0]
    dt, ds = teacher_states.shape[1], hidden_states.shape[1]
    rows = hidden_states.shape[0] // 2
    unit = rows // 8
    half = tokens // 4

    def swap(array):
        return permute(array, lambda y, z, x, c: (y, z, x, 1 - c))

    kx, kz, i = row_parts(rows, 4, 2, unit)
    source = (((x + sign * kx) % 4 * 2 + (zh ^ kz)) * 2 + c) * unit + i
    select = pick(source, 2 * rows).astype(BF16)
    own = jnp.concatenate(
        [
            jnp.dot(select, states, preferred_element_type=F32).astype(BF16)
            for states in (teacher_states, hidden_states)
        ],
        axis=1,
    )
    student_other = swap(student_head)

    from_y = moved(("y", "y"), -1)
    from_z = moved(("z", "z"), -1)
    tied = lax.optimization_barrier
    own_states = own[:unit, dt:].astype(F32)
    y1, z0, own_states, student_other, head_t = tied(
        (permute(own, from_y), permute(own, from_z), own_states, student_other, teacher_head)
    )
    teacher_other = swap(head_t)
    heads_s = resident(student_head, student_other)
    y2, z1, heads_s = tied((permute(y1, from_y), permute(y1, from_z), heads_s))
    gain_row = final_gain[None]
    heads = (teacher_head, heads_s[0], teacher_other, heads_s[1])
    y3, z2 = permute(y2, from_y), permute(y2, from_z)
    half_0 = logits([own, z0, y1, z1], gain_row, *heads)
    y3, z2, half_0 = tied((y3, z2, half_0))
    z3_t, z3_h = permute(y3[:, :dt], from_z), permute(z2[:, dt:], from_y)
    half_1 = logits([y2, z2, y3, z3_t, z3_h], gain_row, *heads)

    ry, rb, kx, kz, i = row_parts(2 * half, 4, 2, 4, 2, unit)
    rz = kz * 2 + rb
    to_y, to_z, to_x = (y + sign * ry) % 4, (z + sign * rz) % 4, (x + sign * kx) % 4
    absolute = (((to_y * 2 + to_z % 2) * 4 + to_x) * 2 + to_z // 2) * unit + i
    order = pick(absolute, 2 * half).astype(F32)
    token = (absolute // unit * 2 + c) * unit + i
    weight = jnp.sum(jnp.where(pick(token, tokens), token_weight[None, :], 0.0), axis=1)

    local = jnp.concatenate([half_0[2][:2], half_1[2][:2]], axis=1)
    whole = jnp.dot(local, order, precision=lax.Precision.HIGHEST)
    for axis in ("x", "y", "z"):
        parts = [whole] + [permute(whole, moved((axis, axis), s)) for s in (1, 3, 2)]
        whole = log_sum(parts)
    relative = jnp.dot(whole, order.T, precision=lax.Precision.HIGHEST)
    rows = jnp.concatenate([relative, weight[None], jnp.zeros((5, 2 * half), F32)], axis=0)

    def exchange(pieces, axis):
        moves = {s: permute(pieces[s - 1], moved((axis, axis), s)) for s in (1, 3, 2)}
        return [moves[s] for s in (1, 2, 3)]

    head_pair = heads_s
    sends_0, kept_0, kept_b, send_b1, gain_0 = backward(
        half_0, rows[:, :half], gain_row, *head_pair
    )
    got_0 = exchange(sends_0, "x")
    got_b1 = permute(send_b1, moved(("y", "y"), 1))
    sends_1, kept_1, send_b2, send_b3, gain = backward(
        half_1, rows[:, half:], gain_row, *head_pair, gain_0
    )
    got_0, sends_1, send_b2, send_b3 = tied((got_0, sends_1, send_b2, send_b3))
    got_1 = exchange(sends_1, "x")
    got_b3 = permute(send_b3, moved(("y", "y"), 3))
    got_b2 = permute(send_b2, moved(("y", "y"), 2))
    wide = ds // 2
    count = half // 8
    kept_a, *sends_a, gain = small(
        between_a,
        [((count, wide), F32)] + [((count, wide + 256), BF16)] * 3 + [(GAIN, F32)],
        *(kept_0, *got_0, kept_1, *got_1, gain),
    )
    got_a = exchange(sends_a, "y")
    kept_b, *sends_b = small(
        between_b,
        [((count, wide), F32)] + [((count, wide), BF16)] * 3,
        *(kept_b, got_b1, got_b2, got_b3),
    )
    got_b = exchange(sends_b, "x")
    kept, *sends, gain = small(
        before_z,
        [((unit, ds), F32)] + [((unit, ds + 1024), BF16)] * 3 + [(GAIN, F32)],
        *(kept_a, *got_a, kept_b, *got_b, gain),
    )
    got = exchange(sends, "z")
    (gain,) = small(last_gain, [(GAIN, F32)], gain, *got)
    gain_grad = (gain + swap(gain)).reshape(-1)[:ds]
    (states_grad,) = small(
        last_states, [((unit, ds), F32)], kept, *got, own_states, gain_row
    )
    return (states_grad, gain_grad)


def solution(mesh):
    torus = Mesh(mesh.devices.reshape(SIZES), AXES)
    return jax.shard_map(
        body,
        mesh=torus,
        in_specs=(
            P(("y", "zl"), None),
            P(),
            P(AXES, None),
            P(("y", "zl"), None),
            P(AXES, None),
            P(),
        ),
        out_specs=(P(AXES, None), P()),
        check_vma=False,
    )
```

```python
import functools

import jax
import jax.numpy as jnp
import numpy as np
from jax import lax
from jax.experimental import pallas as pl
from jax.experimental.pallas import tpu as pltpu
from jax.sharding import Mesh, PartitionSpec as P

EPSILON = 1e-06
AXES = ("y", "zl", "x", "zh", "c")
SIZES = (4, 2, 4, 2, 2)
F32 = jnp.float32
BF16 = jnp.bfloat16
LARGE = 22 * 2**20
SMALL = 4 * 2**20
GAIN = (32, 128)
STEPS_Y = (0, 0, 1, 3, 2, 1, 2, 3)
ACROSS_Z = (0, 1, 0, 0, 0, 1, 1, 1)


def place(y, z, x, c):
    y, z, x, c = y % 4, z % 4, x % 4, c % 2
    return (((y * 2 + z % 2) * 4 + x) * 2 + z // 2) * 2 + c


def permute(array, target):
    pairs = [
        (place(y, z, x, c), place(*target(y, z, x, c)))
        for y in range(4)
        for z in range(4)
        for x in range(4)
        for c in range(2)
    ]
    return lax.ppermute(array, AXES, pairs)


def moved(axis, steps):
    def target(y, z, x, c):
        by = steps if c == 0 else -steps
        name = axis[c]
        return (y + by * (name == "y"), z + by * (name == "z"), x + by * (name == "x"), c)

    return target


def pick(rows, columns):
    return rows[:, None] == lax.broadcasted_iota(jnp.int32, (rows.shape[0], columns), 1)


def row_parts(count, *sizes):
    index = lax.iota(jnp.int32, count)
    digits = []
    for size in reversed(sizes):
        digits.append(index % size)
        index = index // size
    return digits[::-1]


def log_sum(parts):
    top = jnp.maximum(jnp.maximum(parts[0], parts[1]), jnp.maximum(parts[2], parts[3]))
    return top + jnp.log(sum(jnp.exp(part - top) for part in parts))


def columns_to_rows(columns):
    rows = columns[0].shape[0]
    wide = jnp.concatenate(
        columns + [jnp.zeros((rows, 128 - len(columns)), F32)], axis=1
    )
    return wide.T[:8]


def rows_to_columns(rows):
    count = rows.shape[1]
    return jnp.concatenate([rows, jnp.zeros((120, count), F32)], axis=0).T


def resident_kernel(*refs):
    count = (len(refs) - 1) // 2
    sem = refs[-1]
    copies = [
        pltpu.make_async_copy(refs[n], refs[count + n], sem.at[n]) for n in range(count)
    ]
    for copy in copies:
        copy.start()
    for copy in copies:
        copy.wait()


def resident(*arrays):
    return pl.pallas_call(
        resident_kernel,
        in_specs=[pl.BlockSpec(memory_space=pl.ANY)] * len(arrays),
        out_specs=[pl.BlockSpec(memory_space=pltpu.VMEM)] * len(arrays),
        out_shape=[pltpu.VMEM(array.shape, array.dtype) for array in arrays],
        scratch_shapes=[pltpu.SemaphoreType.DMA((len(arrays),))],
        compiler_params=pltpu.CompilerParams(vmem_limit_bytes=SMALL),
        cost_estimate=pl.CostEstimate(
            flops=0, bytes_accessed=4 * sum(a.size for a in arrays), transcendentals=0
        ),
    )(*arrays)


def logits_kernel(tile, *refs):
    starts, blocks, refs = refs[0], refs[1:-12], refs[-12:]
    gain, own_t, own_s, other_t, other_s, out_t, out_s, lse, normed, states_t, wait, sem = refs
    rows, vocab, dt = blocks[0].shape[0], own_t.shape[0], own_t.shape[1]
    slots = wait.shape[0]
    copies = [
        pltpu.make_async_copy(
            head.at[pl.ds(first, tile)], wait.at[n % slots], sem.at[n % slots]
        )
        for n, (head, first) in enumerate(
            (head, first) for head in (own_t, other_t) for first in range(0, vocab, tile)
        )
    ]
    for n in range(slots):
        copies[n].start()
    group = rows // 4
    for k in range(4):
        block = blocks[k]
        wide = block[:, dt:].astype(F32)
        inverse = lax.rsqrt(jnp.mean(wide * wide, axis=1, keepdims=True) + EPSILON)
        made = (wide * inverse * gain[...]).astype(BF16)
        if k < 3:
            span = pl.ds(pl.multiple_of(starts[k], rows), rows)
            states_t[span, :] = block[:, :dt]
            normed[span, :] = made
        else:
            for n in range(4):
                span = pl.ds(pl.multiple_of(starts[k + n], group), group)
                states_t[span, :] = block[n * group : (n + 1) * group, :dt]
                normed[span, :] = made[n * group : (n + 1) * group]
    count = states_t.shape[0]

    def statistics(out, n, top, total):
        part = out[:, pl.ds(n * tile, tile)]
        new = jnp.maximum(top, jnp.max(part, axis=1, keepdims=True))
        total = total * jnp.exp(top - new) + jnp.sum(
            jnp.exp(part - new), axis=1, keepdims=True
        )
        return new, total

    sums = []
    for states, out in ((normed, out_s), (states_t, out_t)):
        top = jnp.full((count, 1), -jnp.inf, F32)
        total = jnp.zeros((count, 1), F32)
        for n in range(2 * vocab // tile):
            if out is out_s:
                head = (own_s, other_s)[n * tile // vocab]
                head = head[pl.ds(n * tile % vocab, tile), :]
            else:
                copies[n].wait()
                head = wait[n % slots]
            out[:, pl.ds(n * tile, tile)] = lax.dot_general(
                states[...], head, (((1,), (1,)), ((), ())), preferred_element_type=F32
            )
            if out is out_t and n + slots < len(copies):
                copies[n + slots].start()
            if n:
                top, total = statistics(out, n - 1, top, total)
        top, total = statistics(out, 2 * vocab // tile - 1, top, total)
        sums.append(top + jnp.log(total))
    lse[...] = columns_to_rows(sums[::-1])


def held(array):
    return pltpu.with_memory_space_constraint(array, pltpu.VMEM)


def away(array):
    return pltpu.with_memory_space_constraint(array, pltpu.HBM)


def logits(starts, blocks, gain, own_t, own_s, other_t, other_s):
    count = 4 * blocks[0].shape[0]
    vocab, dt = own_t.shape
    ds = own_s.shape[1]
    tile, slots = 512, 2
    vmem = pl.BlockSpec(memory_space=pltpu.VMEM)
    anywhere = pl.BlockSpec(memory_space=pl.ANY)
    return pl.pallas_call(
        functools.partial(logits_kernel, tile),
        in_specs=[pl.BlockSpec(memory_space=pltpu.SMEM)]
        + [vmem] * (len(blocks) + 1)
        + [anywhere, vmem] * 2,
        out_specs=[vmem] * 4,
        out_shape=[
            jax.ShapeDtypeStruct((count, 2 * vocab), F32),
            jax.ShapeDtypeStruct((count, 2 * vocab), F32),
            jax.ShapeDtypeStruct((8, count), F32),
            jax.ShapeDtypeStruct((count, ds), BF16),
        ],
        scratch_shapes=[
            pltpu.VMEM((count, dt), BF16),
            pltpu.VMEM((slots, tile, dt), BF16),
            pltpu.SemaphoreType.DMA((slots,)),
        ],
        compiler_params=pltpu.CompilerParams(vmem_limit_bytes=LARGE),
        cost_estimate=pl.CostEstimate(
            flops=4 * count * vocab * (dt + ds),
            bytes_accessed=4 * vocab * (dt + ds),
            transcendentals=4 * vocab * count,
        ),
    )(starts, *blocks, gain, away(own_t), held(own_s), away(other_t), held(other_s))


def backward_kernel(tile, *refs):
    halves, (rows, gain, own, other) = (refs[0:3], refs[3:6]), refs[6:10]
    sends_a, kept_a, sends_b, kept_b = refs[10:13], refs[13], refs[14:17], refs[17]
    gain_out, grad = refs[18:]
    half, vocab = halves[0][0].shape
    part, ds = own.shape
    steps = ds // tile
    columns = rows_to_columns(rows[...])
    for n, (teacher, student, _) in enumerate(halves):
        span = slice(n * half, (n + 1) * half)
        lse_t, lse_s, weight = (columns[span, k : k + 1] for k in range(3))
        for first in range(0, vocab, 512):
            at = pl.ds(first, 512)
            gap = jnp.exp(student[:, at] - lse_s) - jnp.exp(teacher[:, at] - lse_t)
            grad[pl.ds(n * half, half), at] = (weight * gap).astype(BF16)
    size = half // 4
    base = {key: size * n for n, key in enumerate(zip(STEPS_Y, ACROSS_Z))}
    for k in range(steps):
        at = pl.ds(k * tile, tile)
        out = jnp.dot(grad[:, :part], own[:, at], preferred_element_type=F32)
        out += jnp.dot(grad[:, part:], other[:, at], preferred_element_type=F32)
        share = sum(
            jnp.sum(
                out[n * half : (n + 1) * half] * normed[:, at].astype(F32),
                axis=0,
                keepdims=True,
            )
            for n, (_, _, normed) in enumerate(halves)
        )
        share /= gain[:, at]
        for n in range(tile // 128):
            gain_out[pl.ds(k * tile // 128 + n, 1), :] = share[:, 128 * n : 128 * (n + 1)]
        second = k >= steps // 2
        at = pl.ds((k - second * (steps // 2)) * tile, tile)
        for s in range(4):
            if second:
                spans = [(base[s, across], size) for across in range(2)]
            else:
                spans = [
                    (base[steps_y, across] + size // 4 * s, size // 4)
                    for steps_y in range(4)
                    for across in range(2)
                ]
            piece = jnp.concatenate([out[f : f + count] for f, count in spans], axis=0)
            if s == 0:
                (kept_a, kept_b)[second][:, at] = piece
            else:
                (sends_a, sends_b)[second][s - 1][:, at] = piece.astype(BF16)
    used = ds // 128
    gain_out[used:, :] = jnp.zeros((gain_out.shape[0] - used, 128), F32)
    tail = packed(gain_out[...], half // 2).astype(BF16)
    for send in sends_a:
        send[:, pl.ds(ds // 2, 128)] = tail


def backward(halves, rows, gain, own, other):
    half, vocab = halves[0][0].shape
    part, ds = own.shape
    tile = ds // 4
    vmem = pl.BlockSpec(memory_space=pltpu.VMEM)
    count, wide = half // 2, ds // 2
    out = pl.pallas_call(
        functools.partial(backward_kernel, tile),
        in_specs=[vmem] * 10,
        out_specs=[vmem] * 9,
        out_shape=[jax.ShapeDtypeStruct((count, wide + 128), BF16)] * 3
        + [jax.ShapeDtypeStruct((count, wide), F32)]
        + [jax.ShapeDtypeStruct((count, wide), BF16)] * 3
        + [jax.ShapeDtypeStruct((count, wide), F32)]
        + [jax.ShapeDtypeStruct(GAIN, F32)],
        scratch_shapes=[pltpu.VMEM((2 * half, vocab), BF16)],
        compiler_params=pltpu.CompilerParams(vmem_limit_bytes=LARGE),
        cost_estimate=pl.CostEstimate(
            flops=4 * half * vocab * ds,
            bytes_accessed=2 * vocab * ds,
            transcendentals=4 * vocab * half,
        ),
    )(
        *(part_of[n] for part_of in halves for n in (0, 1, 3)),
        *(rows, gain, held(own), held(other)),
    )
    return out[:3], out[3], out[4:7], out[7], out[8]


def packed(gain, rows):
    high = gain.astype(BF16).astype(F32)
    parts = jnp.concatenate([high, gain - high], axis=0)
    count = parts.shape[0]
    if rows > count:
        return jnp.concatenate([parts, jnp.zeros((rows - count, 128), F32)], axis=0)
    return jnp.concatenate(
        [parts[first : first + rows] for first in range(0, count, rows)], axis=1
    )


def unpacked(tail):
    tail = tail.astype(F32)
    parts = jnp.concatenate(
        [tail[:, first : first + 128] for first in range(0, tail.shape[1], 128)], axis=0
    )
    half = GAIN[0]
    return parts[:half] + parts[half : 2 * half]


def small(kernel, out_shape, *args):
    vmem = pl.BlockSpec(memory_space=pltpu.VMEM)
    return pl.pallas_call(
        kernel,
        in_specs=[vmem] * len(args),
        out_specs=[vmem] * len(out_shape),
        out_shape=[jax.ShapeDtypeStruct(*shape) for shape in out_shape],
        compiler_params=pltpu.CompilerParams(vmem_limit_bytes=SMALL),
    )(*args)


def added(kept, pieces):
    wide = kept.shape[1]
    first, second, third = (piece[:, :wide].astype(F32) for piece in pieces)
    return (kept[...] + first) + (second + third)


def added_gain(gain, pieces, wide):
    first, second, third = (unpacked(piece[:, wide:]) for piece in pieces)
    return (gain[...] + first) + (second + third)


def between_a(*refs):
    kept_a, got, gain, kept, sends, gain_out = refs[0], refs[1:4], refs[4], refs[5], refs[6:9], refs[9]
    count = kept.shape[0]
    total = added(kept_a, got)
    share = added_gain(gain, got, kept_a.shape[1])
    gain_out[...] = share
    tail = packed(share, count)
    kept[...] = total[:count]
    for s, send in enumerate(sends, 1):
        piece = total[s * count : (s + 1) * count]
        send[...] = jnp.concatenate([piece, tail], axis=1).astype(BF16)


def between_b(*refs):
    total = added(refs[0], refs[1:4])
    half = total.shape[0] // 2
    for s in range(4):
        piece = jnp.concatenate(
            [total[n * half + 16 * s : n * half + 16 * s + 16] for n in range(2)], axis=0
        )
        refs[4 + s][...] = piece.astype(refs[4 + s].dtype)


def before_z(*refs):
    kept_a, got_a, kept_b, got_b, gain = refs[0], refs[1:4], refs[4], refs[5:8], refs[8]
    kept, sends, gain_out = refs[9], refs[10:13], refs[13]
    rows, wide = kept_a.shape
    unit = rows // 4
    total = jnp.concatenate([added(kept_a, got_a), added(kept_b, got_b)], axis=1)
    share = added_gain(gain, got_a, wide)
    gain_out[...] = share
    tail = packed(share, unit)
    kept[...] = total[:unit]
    for send, n in zip(sends, (2, 1, 3)):
        piece = total[n * unit : (n + 1) * unit]
        send[...] = jnp.concatenate([piece, tail], axis=1).astype(BF16)


def last_gain(gain, first, second, third, out):
    wide = first.shape[1] - 2 * gain.size // first.shape[0]
    out[...] = added_gain(gain, (first, second, third), wide)


def last_states(kept, first, second, third, states, gain, out):
    total = added(kept, (first, second, third))
    own = states[...]
    inverse = lax.rsqrt(jnp.mean(own * own, axis=1, keepdims=True) + EPSILON)
    scaled = total * gain[...]
    out[...] = inverse * scaled - own * (inverse * inverse * inverse) * jnp.mean(
        own * scaled, axis=1, keepdims=True
    )


def body(hidden_states, final_gain, student_head, teacher_states, teacher_head, token_weight):
    y, zl, x, zh, c = (lax.axis_index(name) for name in AXES)
    z = zh * 2 + zl
    sign = 1 - 2 * c
    tokens = token_weight.shape[0]
    dt, ds = teacher_states.shape[1], hidden_states.shape[1]
    rows = hidden_states.shape[0] // 2
    unit = rows // 8
    half = tokens // 4

    def swap(array):
        return permute(array, lambda y, z, x, c: (y, z, x, 1 - c))

    kx, kz, i = row_parts(rows, 4, 2, unit)
    source = (((x + sign * kx) % 4 * 2 + (zh ^ kz)) * 2 + c) * unit + i
    select = pick(source, 2 * rows).astype(BF16)
    own = jnp.concatenate(
        [
            jnp.dot(select, states, preferred_element_type=F32).astype(BF16)
            for states in (teacher_states, hidden_states)
        ],
        axis=1,
    )
    student_other = swap(student_head)

    def from_y(y, z, x, c):
        return (y - (1 - 2 * c) * (1 - 2 * (x % 2)), z, x, c)

    def trade(y, z, x, c):
        return (y, z, x + (1 - 2 * c) * (1 - 2 * (x % 2)), c)

    from_z = moved(("z", "z"), -1)
    tied = lax.optimization_barrier
    own_states = own[:unit, dt:].astype(F32)
    walked, z0, own_states, student_other, head_t = tied(
        (permute(own, from_y), permute(own, from_z), own_states, student_other, teacher_head)
    )
    teacher_other = swap(head_t)
    y2, across, traded, head_s = tied(
        (permute(walked, from_y), permute(walked, from_z), permute(walked, trade), student_head)
    )
    heads_s = resident(away(head_s), away(student_other))
    gain_row = final_gain[None]
    heads = (teacher_head, heads_s[0], teacher_other, heads_s[1])
    odd = x % 2
    z2, across_traded = permute(y2, from_z), permute(across, trade)
    turn = (lax.iota(jnp.int32, 4) + 1 - 2 * odd) % 4 * (rows // 4)

    def starts(first, second, third, fourth):
        fixed = jnp.stack([0 * odd + first, 0 * odd + second, 0 * odd + third])
        return jnp.concatenate([rows * fixed, rows * fourth + turn])

    half_0 = logits(
        starts(0, 1, 2 + odd, 3 - odd), [own, z0, walked, traded], gain_row, *heads
    )
    z2, across_traded, half_0 = tied((z2, across_traded, half_0))
    half_1 = logits(
        starts(0, 1 + 2 * odd, 2, 3 - 2 * odd),
        [y2, across, z2, across_traded],
        gain_row,
        *heads,
    )

    _, kx, kz, i = row_parts(2 * half, 8, 4, 2, unit)
    ry, rb = (np.repeat(np.array(t, np.int32), rows) for t in (STEPS_Y, ACROSS_Z))
    rz = kz * 2 + rb
    to_y, to_z, to_x = (y + sign * ry) % 4, (z + sign * rz) % 4, (x + sign * kx) % 4
    absolute = (((to_y * 2 + to_z % 2) * 4 + to_x) * 2 + to_z // 2) * unit + i
    order = pick(absolute, 2 * half).astype(F32)
    token = (absolute // unit * 2 + c) * unit + i
    weight = jnp.sum(jnp.where(pick(token, tokens), token_weight[None, :], 0.0), axis=1)

    local = jnp.concatenate([half_0[2][:2], half_1[2][:2]], axis=1)
    whole = jnp.dot(local, order, precision=lax.Precision.HIGHEST)
    for axis in ("x", "y", "z"):
        parts = [whole] + [permute(whole, moved((axis, axis), s)) for s in (1, 3, 2)]
        whole = log_sum(parts)
    relative = jnp.dot(whole, order.T, precision=lax.Precision.HIGHEST)
    rows_in = jnp.concatenate(
        [relative, weight[None], jnp.zeros((5, 2 * half), F32)], axis=0
    )

    def exchange(pieces, axis):
        moves = {s: permute(pieces[s - 1], moved((axis, axis), s)) for s in (1, 3, 2)}
        return [moves[s] for s in (1, 2, 3)]

    sends_a, kept_a, sends_b, kept_b, gain = backward(
        (half_0, half_1), rows_in, gain_row, *heads_s
    )
    got_a, got_b = exchange(sends_a, "x"), exchange(sends_b, "y")
    wide = ds // 2
    count = half // 8
    kept_a, *sends_a, gain = small(
        between_a,
        [((count, wide), F32)] + [((count, wide + 256), BF16)] * 3 + [(GAIN, F32)],
        *(kept_a, *got_a, gain),
    )
    got_a = exchange(sends_a, "y")
    kept_b, *sends_b = small(
        between_b,
        [((count, wide), F32)] + [((count, wide), BF16)] * 3,
        *(kept_b, *got_b),
    )
    got_b = exchange(sends_b, "x")
    kept, *sends, gain = small(
        before_z,
        [((unit, ds), F32)] + [((unit, ds + 1024), BF16)] * 3 + [(GAIN, F32)],
        *(kept_a, *got_a, kept_b, *got_b, gain),
    )
    got = exchange(sends, "z")
    (gain,) = small(last_gain, [(GAIN, F32)], gain, *got)
    gain_grad = (gain + swap(gain)).reshape(-1)[:ds]
    (states_grad,) = small(
        last_states, [((unit, ds), F32)], kept, *got, own_states, gain_row
    )
    return (states_grad, gain_grad)


def solution(mesh):
    torus = Mesh(mesh.devices.reshape(SIZES), AXES)
    return jax.shard_map(
        body,
        mesh=torus,
        in_specs=(
            P(("y", "zl"), None),
            P(),
            P(AXES, None),
            P(("y", "zl"), None),
            P(AXES, None),
            P(),
        ),
        out_specs=(P(AXES, None), P()),
        check_vma=False,
    )
```

```python
import functools

import jax
import jax.numpy as jnp
import numpy as np
from jax import lax
from jax.experimental import pallas as pl
from jax.experimental.pallas import tpu as pltpu
from jax.sharding import Mesh, PartitionSpec as P

EPSILON = 1e-06
AXES = ("y", "zl", "x", "zh", "c")
SIZES = (4, 2, 4, 2, 2)
F32 = jnp.float32
BF16 = jnp.bfloat16
LARGE = 22 * 2**20
SMALL = 4 * 2**20
GAIN = (32, 128)
STEPS_Y = (0, 0, 1, 3, 2, 1, 2, 3)
ACROSS_Z = (0, 1, 0, 0, 0, 1, 1, 1)


def place(y, z, x, c):
    y, z, x, c = y % 4, z % 4, x % 4, c % 2
    return (((y * 2 + z % 2) * 4 + x) * 2 + z // 2) * 2 + c


def permute(array, target):
    pairs = [
        (place(y, z, x, c), place(*target(y, z, x, c)))
        for y in range(4)
        for z in range(4)
        for x in range(4)
        for c in range(2)
    ]
    return lax.ppermute(array, AXES, pairs)


def moved(axis, steps):
    def target(y, z, x, c):
        by = steps if c == 0 else -steps
        name = axis[c]
        return (y + by * (name == "y"), z + by * (name == "z"), x + by * (name == "x"), c)

    return target


def pick(rows, columns):
    return rows[:, None] == lax.broadcasted_iota(jnp.int32, (rows.shape[0], columns), 1)


def row_parts(count, *sizes):
    index = lax.iota(jnp.int32, count)
    digits = []
    for size in reversed(sizes):
        digits.append(index % size)
        index = index // size
    return digits[::-1]


def log_sum(parts):
    top = jnp.maximum(jnp.maximum(parts[0], parts[1]), jnp.maximum(parts[2], parts[3]))
    return top + jnp.log(sum(jnp.exp(part - top) for part in parts))


def columns_to_rows(columns):
    rows = columns[0].shape[0]
    wide = jnp.concatenate(
        columns + [jnp.zeros((rows, 128 - len(columns)), F32)], axis=1
    )
    return wide.T[:8]


def rows_to_columns(rows):
    count = rows.shape[1]
    return jnp.concatenate([rows, jnp.zeros((120, count), F32)], axis=0).T


def resident_kernel(*refs):
    count = (len(refs) - 1) // 2
    sem = refs[-1]
    copies = [
        pltpu.make_async_copy(refs[n], refs[count + n], sem.at[n]) for n in range(count)
    ]
    for copy in copies:
        copy.start()
    for copy in copies:
        copy.wait()


def resident(*arrays):
    return pl.pallas_call(
        resident_kernel,
        in_specs=[pl.BlockSpec(memory_space=pl.ANY)] * len(arrays),
        out_specs=[pl.BlockSpec(memory_space=pltpu.VMEM)] * len(arrays),
        out_shape=[pltpu.VMEM(array.shape, array.dtype) for array in arrays],
        scratch_shapes=[pltpu.SemaphoreType.DMA((len(arrays),))],
        compiler_params=pltpu.CompilerParams(vmem_limit_bytes=SMALL),
        cost_estimate=pl.CostEstimate(
            flops=0, bytes_accessed=4 * sum(a.size for a in arrays), transcendentals=0
        ),
    )(*arrays)


def logits_kernel(tile, *refs):
    starts, blocks, refs = refs[0], refs[1:-12], refs[-12:]
    gain, own_t, own_s, other_t, other_s, out_t, out_s, lse, normed, states_t, wait, sem = refs
    rows, vocab, dt = blocks[0].shape[0], own_t.shape[0], own_t.shape[1]
    slots = wait.shape[0]
    copies = [
        pltpu.make_async_copy(
            head.at[pl.ds(first, tile)], wait.at[n % slots], sem.at[n % slots]
        )
        for n, (head, first) in enumerate(
            (head, first) for head in (own_t, other_t) for first in range(0, vocab, tile)
        )
    ]
    for n in range(slots):
        copies[n].start()
    group = rows // 4
    for k in range(4):
        block = blocks[k]
        wide = block[:, dt:].astype(F32)
        inverse = lax.rsqrt(jnp.mean(wide * wide, axis=1, keepdims=True) + EPSILON)
        made = (wide * inverse * gain[...]).astype(BF16)
        if k < 3:
            span = pl.ds(pl.multiple_of(starts[k], rows), rows)
            states_t[span, :] = block[:, :dt]
            normed[span, :] = made
        else:
            for n in range(4):
                span = pl.ds(pl.multiple_of(starts[k + n], group), group)
                states_t[span, :] = block[n * group : (n + 1) * group, :dt]
                normed[span, :] = made[n * group : (n + 1) * group]
    count = states_t.shape[0]

    def statistics(out, n, top, total):
        part = out[:, pl.ds(n * tile, tile)]
        new = jnp.maximum(top, jnp.max(part, axis=1, keepdims=True))
        total = total * jnp.exp(top - new) + jnp.sum(
            jnp.exp(part - new), axis=1, keepdims=True
        )
        return new, total

    sums = []
    for states, out in ((normed, out_s), (states_t, out_t)):
        top = jnp.full((count, 1), -jnp.inf, F32)
        total = jnp.zeros((count, 1), F32)
        for n in range(2 * vocab // tile):
            if out is out_s:
                head = (own_s, other_s)[n * tile // vocab]
                head = head[pl.ds(n * tile % vocab, tile), :]
            else:
                copies[n].wait()
                head = wait[n % slots]
            out[:, pl.ds(n * tile, tile)] = lax.dot_general(
                states[...], head, (((1,), (1,)), ((), ())), preferred_element_type=F32
            )
            if out is out_t and n + slots < len(copies):
                copies[n + slots].start()
            if n:
                top, total = statistics(out, n - 1, top, total)
        top, total = statistics(out, 2 * vocab // tile - 1, top, total)
        sums.append(top + jnp.log(total))
    lse[...] = columns_to_rows(sums[::-1])


def held(array):
    return pltpu.with_memory_space_constraint(array, pltpu.VMEM)


def away(array):
    return pltpu.with_memory_space_constraint(array, pltpu.HBM)


def logits(starts, blocks, gain, own_t, own_s, other_t, other_s):
    count = 4 * blocks[0].shape[0]
    vocab, dt = own_t.shape
    ds = own_s.shape[1]
    tile, slots = 512, 2
    vmem = pl.BlockSpec(memory_space=pltpu.VMEM)
    anywhere = pl.BlockSpec(memory_space=pl.ANY)
    return pl.pallas_call(
        functools.partial(logits_kernel, tile),
        in_specs=[pl.BlockSpec(memory_space=pltpu.SMEM)]
        + [vmem] * (len(blocks) + 1)
        + [anywhere, vmem] * 2,
        out_specs=[vmem] * 4,
        out_shape=[
            jax.ShapeDtypeStruct((count, 2 * vocab), F32),
            jax.ShapeDtypeStruct((count, 2 * vocab), F32),
            jax.ShapeDtypeStruct((8, count), F32),
            jax.ShapeDtypeStruct((count, ds), BF16),
        ],
        scratch_shapes=[
            pltpu.VMEM((count, dt), BF16),
            pltpu.VMEM((slots, tile, dt), BF16),
            pltpu.SemaphoreType.DMA((slots,)),
        ],
        compiler_params=pltpu.CompilerParams(vmem_limit_bytes=LARGE),
        cost_estimate=pl.CostEstimate(
            flops=4 * count * vocab * (dt + ds),
            bytes_accessed=4 * vocab * (dt + ds),
            transcendentals=4 * vocab * count,
        ),
    )(starts, *blocks, gain, away(own_t), held(own_s), away(other_t), held(other_s))


def backward_kernel(tile, *refs):
    halves, (rows, gain, own, other) = (refs[0:3], refs[3:6]), refs[6:10]
    sends_a, kept_a, sends_b, kept_b = refs[10:13], refs[13], refs[14:17], refs[17]
    gain_out, grad = refs[18:]
    half, vocab = halves[0][0].shape
    part, ds = own.shape
    steps = ds // tile
    columns = rows_to_columns(rows[...])
    for n, (teacher, student, _) in enumerate(halves):
        span = slice(n * half, (n + 1) * half)
        lse_t, lse_s, weight = (columns[span, k : k + 1] for k in range(3))
        for first in range(0, vocab, 512):
            at = pl.ds(first, 512)
            gap = jnp.exp(student[:, at] - lse_s) - jnp.exp(teacher[:, at] - lse_t)
            grad[pl.ds(n * half, half), at] = (weight * gap).astype(BF16)
    size = half // 4
    base = {key: size * n for n, key in enumerate(zip(STEPS_Y, ACROSS_Z))}
    for k in range(steps):
        at = pl.ds(k * tile, tile)
        out = jnp.dot(grad[:, :part], own[:, at], preferred_element_type=F32)
        out += jnp.dot(grad[:, part:], other[:, at], preferred_element_type=F32)
        share = sum(
            jnp.sum(
                out[n * half : (n + 1) * half] * normed[:, at].astype(F32),
                axis=0,
                keepdims=True,
            )
            for n, (_, _, normed) in enumerate(halves)
        )
        share /= gain[:, at]
        for n in range(tile // 128):
            gain_out[pl.ds(k * tile // 128 + n, 1), :] = share[:, 128 * n : 128 * (n + 1)]
        second = k >= steps // 2
        at = pl.ds((k - second * (steps // 2)) * tile, tile)
        for s in range(4):
            if second:
                spans = [(base[s, across], size) for across in range(2)]
            else:
                spans = [
                    (base[steps_y, across] + size // 4 * s, size // 4)
                    for steps_y in range(4)
                    for across in range(2)
                ]
            piece = jnp.concatenate([out[f : f + count] for f, count in spans], axis=0)
            if s == 0:
                (kept_a, kept_b)[second][:, at] = piece
            else:
                (sends_a, sends_b)[second][s - 1][:, at] = piece.astype(BF16)
    used = ds // 128
    gain_out[used:, :] = jnp.zeros((gain_out.shape[0] - used, 128), F32)
    tail = packed(gain_out[...], half // 2).astype(BF16)
    for send in sends_a:
        send[:, pl.ds(ds // 2, 128)] = tail


def backward(halves, rows, gain, own, other):
    half, vocab = halves[0][0].shape
    part, ds = own.shape
    tile = ds // 4
    vmem = pl.BlockSpec(memory_space=pltpu.VMEM)
    count, wide = half // 2, ds // 2
    out = pl.pallas_call(
        functools.partial(backward_kernel, tile),
        in_specs=[vmem] * 10,
        out_specs=[vmem] * 9,
        out_shape=[jax.ShapeDtypeStruct((count, wide + 128), BF16)] * 3
        + [jax.ShapeDtypeStruct((count, wide), F32)]
        + [jax.ShapeDtypeStruct((count, wide), BF16)] * 3
        + [jax.ShapeDtypeStruct((count, wide), F32)]
        + [jax.ShapeDtypeStruct(GAIN, F32)],
        scratch_shapes=[pltpu.VMEM((2 * half, vocab), BF16)],
        compiler_params=pltpu.CompilerParams(vmem_limit_bytes=LARGE),
        cost_estimate=pl.CostEstimate(
            flops=4 * half * vocab * ds,
            bytes_accessed=2 * vocab * ds,
            transcendentals=4 * vocab * half,
        ),
    )(
        *(part_of[n] for part_of in halves for n in (0, 1, 3)),
        *(rows, gain, held(own), held(other)),
    )
    return out[:3], out[3], out[4:7], out[7], out[8]


def packed(gain, rows):
    high = gain.astype(BF16).astype(F32)
    parts = jnp.concatenate([high, gain - high], axis=0)
    count = parts.shape[0]
    if rows > count:
        return jnp.concatenate([parts, jnp.zeros((rows - count, 128), F32)], axis=0)
    return jnp.concatenate(
        [parts[first : first + rows] for first in range(0, count, rows)], axis=1
    )


def unpacked(tail):
    tail = tail.astype(F32)
    parts = jnp.concatenate(
        [tail[:, first : first + 128] for first in range(0, tail.shape[1], 128)], axis=0
    )
    half = GAIN[0]
    return parts[:half] + parts[half : 2 * half]


def small(kernel, out_shape, *args):
    vmem = pl.BlockSpec(memory_space=pltpu.VMEM)
    return pl.pallas_call(
        kernel,
        in_specs=[vmem] * len(args),
        out_specs=[vmem] * len(out_shape),
        out_shape=[jax.ShapeDtypeStruct(*shape) for shape in out_shape],
        compiler_params=pltpu.CompilerParams(vmem_limit_bytes=SMALL),
    )(*args)


def added(kept, pieces):
    wide = kept.shape[1]
    first, second, third = (piece[:, :wide].astype(F32) for piece in pieces)
    return (kept[...] + first) + (second + third)


def added_gain(gain, pieces, wide):
    first, second, third = (unpacked(piece[:, wide:]) for piece in pieces)
    return (gain[...] + first) + (second + third)


def between_a(*refs):
    kept_a, got, gain, kept, sends, gain_out = refs[0], refs[1:4], refs[4], refs[5], refs[6:9], refs[9]
    count = kept.shape[0]
    total = added(kept_a, got)
    share = added_gain(gain, got, kept_a.shape[1])
    gain_out[...] = share
    tail = packed(share, count)
    kept[...] = total[:count]
    for s, send in enumerate(sends, 1):
        piece = total[s * count : (s + 1) * count]
        send[...] = jnp.concatenate([piece, tail], axis=1).astype(BF16)


def between_b(*refs):
    total = added(refs[0], refs[1:4])
    half = total.shape[0] // 2
    for s in range(4):
        piece = jnp.concatenate(
            [total[n * half + 16 * s : n * half + 16 * s + 16] for n in range(2)], axis=0
        )
        refs[4 + s][...] = piece.astype(refs[4 + s].dtype)


def before_z(*refs):
    kept_a, got_a, kept_b, got_b, gain = refs[0], refs[1:4], refs[4], refs[5:8], refs[8]
    kept, sends, gain_out = refs[9], refs[10:13], refs[13]
    rows, wide = kept_a.shape
    unit = rows // 4
    total = jnp.concatenate([added(kept_a, got_a), added(kept_b, got_b)], axis=1)
    share = added_gain(gain, got_a, wide)
    gain_out[...] = share
    tail = packed(share, unit)
    kept[...] = total[:unit]
    for send, n in zip(sends, (2, 1, 3)):
        piece = total[n * unit : (n + 1) * unit]
        send[...] = jnp.concatenate([piece, tail], axis=1).astype(BF16)


def last_gain(gain, first, second, third, out):
    wide = first.shape[1] - 2 * gain.size // first.shape[0]
    out[...] = added_gain(gain, (first, second, third), wide)


def last_states(kept, first, second, third, states, gain, out):
    total = added(kept, (first, second, third))
    own = states[...]
    inverse = lax.rsqrt(jnp.mean(own * own, axis=1, keepdims=True) + EPSILON)
    scaled = total * gain[...]
    out[...] = inverse * scaled - own * (inverse * inverse * inverse) * jnp.mean(
        own * scaled, axis=1, keepdims=True
    )


def body(hidden_states, final_gain, student_head, teacher_states, teacher_head, token_weight):
    y, zl, x, zh, c = (lax.axis_index(name) for name in AXES)
    z = zh * 2 + zl
    sign = 1 - 2 * c
    tokens = token_weight.shape[0]
    dt, ds = teacher_states.shape[1], hidden_states.shape[1]
    rows = hidden_states.shape[0] // 2
    unit = rows // 8
    half = tokens // 4

    def swap(array):
        return permute(array, lambda y, z, x, c: (y, z, x, 1 - c))

    kx, kz, i = row_parts(rows, 4, 2, unit)
    source = (((x + sign * kx) % 4 * 2 + (zh ^ kz)) * 2 + c) * unit + i
    select = pick(source, 2 * rows).astype(BF16)
    own = jnp.concatenate(
        [
            jnp.dot(select, states, preferred_element_type=F32).astype(BF16)
            for states in (teacher_states, hidden_states)
        ],
        axis=1,
    )
    student_other = swap(student_head)

    def from_y(y, z, x, c):
        return (y - (1 - 2 * c) * (1 - 2 * (x % 2)), z, x, c)

    def trade(y, z, x, c):
        return (y, z, x + (1 - 2 * c) * (1 - 2 * (x % 2)), c)

    from_z = moved(("z", "z"), -1)
    tied = lax.optimization_barrier
    own_states = own[:unit, dt:].astype(F32)
    walked, z0, own_states, student_other, head_t = tied(
        (permute(own, from_y), permute(own, from_z), own_states, student_other, teacher_head)
    )
    teacher_other = swap(head_t)
    heads_s = resident(away(student_head), away(student_other))
    y2, across, traded, heads_s = tied(
        (permute(walked, from_y), permute(walked, from_z), permute(walked, trade), heads_s)
    )
    gain_row = final_gain[None]
    heads = (teacher_head, heads_s[0], teacher_other, heads_s[1])
    odd = x % 2
    z2, across_traded = permute(y2, from_z), permute(across, trade)
    turn = (lax.iota(jnp.int32, 4) + 1 - 2 * odd) % 4 * (rows // 4)

    def starts(first, second, third, fourth):
        fixed = jnp.stack([0 * odd + first, 0 * odd + second, 0 * odd + third])
        return jnp.concatenate([rows * fixed, rows * fourth + turn])

    half_0 = logits(
        starts(0, 1, 2 + odd, 3 - odd), [own, z0, walked, traded], gain_row, *heads
    )
    z2, across_traded, half_0 = tied((z2, across_traded, half_0))
    half_1 = logits(
        starts(0, 1 + 2 * odd, 2, 3 - 2 * odd),
        [y2, across, z2, across_traded],
        gain_row,
        *heads,
    )

    _, kx, kz, i = row_parts(2 * half, 8, 4, 2, unit)
    ry, rb = (np.repeat(np.array(t, np.int32), rows) for t in (STEPS_Y, ACROSS_Z))
    rz = kz * 2 + rb
    to_y, to_z, to_x = (y + sign * ry) % 4, (z + sign * rz) % 4, (x + sign * kx) % 4
    absolute = (((to_y * 2 + to_z % 2) * 4 + to_x) * 2 + to_z // 2) * unit + i
    order = pick(absolute, 2 * half).astype(F32)
    token = (absolute // unit * 2 + c) * unit + i
    weight = jnp.sum(jnp.where(pick(token, tokens), token_weight[None, :], 0.0), axis=1)

    local = jnp.concatenate([half_0[2][:2], half_1[2][:2]], axis=1)
    whole = jnp.dot(local, order, precision=lax.Precision.HIGHEST)
    for axis in ("x", "y", "z"):
        parts = [whole] + [permute(whole, moved((axis, axis), s)) for s in (1, 3, 2)]
        whole = log_sum(parts)
    relative = jnp.dot(whole, order.T, precision=lax.Precision.HIGHEST)
    rows_in = jnp.concatenate(
        [relative, weight[None], jnp.zeros((5, 2 * half), F32)], axis=0
    )

    def exchange(pieces, axis):
        moves = {s: permute(pieces[s - 1], moved((axis, axis), s)) for s in (1, 3, 2)}
        return [moves[s] for s in (1, 2, 3)]

    sends_a, kept_a, sends_b, kept_b, gain = backward(
        (half_0, half_1), rows_in, gain_row, *heads_s
    )
    got_a, got_b = exchange(sends_a, "x"), exchange(sends_b, "y")
    wide = ds // 2
    count = half // 8
    kept_a, *sends_a, gain = small(
        between_a,
        [((count, wide), F32)] + [((count, wide + 256), BF16)] * 3 + [(GAIN, F32)],
        *(kept_a, *got_a, gain),
    )
    got_a = exchange(sends_a, "y")
    kept_b, *sends_b = small(
        between_b,
        [((count, wide), F32)] + [((count, wide), BF16)] * 3,
        *(kept_b, *got_b),
    )
    got_b = exchange(sends_b, "x")
    kept, *sends, gain = small(
        before_z,
        [((unit, ds), F32)] + [((unit, ds + 1024), BF16)] * 3 + [(GAIN, F32)],
        *(kept_a, *got_a, kept_b, *got_b, gain),
    )
    got = exchange(sends, "z")
    (gain,) = small(last_gain, [(GAIN, F32)], gain, *got)
    gain_grad = (gain + swap(gain)).reshape(-1)[:ds]
    (states_grad,) = small(
        last_states, [((unit, ds), F32)], kept, *got, own_states, gain_row
    )
    return (states_grad, gain_grad)


def solution(mesh):
    torus = Mesh(mesh.devices.reshape(SIZES), AXES)
    return jax.shard_map(
        body,
        mesh=torus,
        in_specs=(
            P(("y", "zl"), None),
            P(),
            P(AXES, None),
            P(("y", "zl"), None),
            P(AXES, None),
            P(),
        ),
        out_specs=(P(AXES, None), P()),
        check_vma=False,
    )
```
